256 devices in a mesh: dp: 32 (over x, z_hi, core), seq: 8 (over z_lo, y).
Axes of the slice: x: 4, y: 4, z: 8 (z_hi: 4, z_lo: 2; z = z_hi * 2 + z_lo), core: 2. Of those that a mesh axis runs over, the one named last changes fastest.
Arguments:
- query_rows: bfloat16 [32768, 1536], P(('dp', 'seq')), may hold values from -6 to 6
- key_rows: bfloat16 [32768, 1536], P(('dp', 'seq')), may hold values from -6 to 6
- value_rows: bfloat16 [32768, 1536], P(('dp', 'seq')), may hold values from -6 to 6
- d_caption: bfloat16 [4096, 1536], P(('dp', 'seq')), may hold values from -6 to 6
- d_image: bfloat16 [28672, 1536], P(('dp', 'seq')), may hold values from -6 to 6
- proj_weight: bfloat16 [1536, 1536], P(('dp', 'seq')), may hold values from -0.15625 to 0.15625
- lengths: int32 [32], P('dp'), may hold values from 224 to 896, as said below
Outputs:
- grad_query: bfloat16 [32768, 1536], P(('dp', 'seq'))
- grad_key: bfloat16 [32768, 1536], P(('dp', 'seq'))
- grad_value: bfloat16 [32768, 1536], P(('dp', 'seq'))
- grad_proj: float32 [1536, 1536], P(('dp', 'seq'))
The draws below stay inside these ranges and needn't reach their ends.
Inputs may be any that keep to these rules, and one draw needn't show every extreme that they name: `lengths`: one sequence has exactly 896 image tokens.
All inputs are finite; a program needn't handle non-finite values.
Results may differ from the reference program's by a relative error of at most 0.019.
Values may be sent and summed in bfloat16 or wider, within the bound.
A program may use at most 64 MiB of HBM per device.

```python
import jax
import jax.numpy as jnp
from jax import lax

HEADS = 12
HD = 128
OUT = 1536
CAP_DEV = 16
IMG_DEV = 112
ATT = 1536
CAPTION = 128
IMAGE = 896
SEQ_LEN = 1024
TOKENS = 32768
CAP_ALL = 4096
IMG_ALL = 28672
N_DP = 32
N_SEQ = 8


def draw_query_rows(key, part):
    key = jax.random.fold_in(key, 11)
    return jnp.clip(jax.random.normal(key, (TOKENS, ATT), jnp.float32), -6.0, 6.0).astype(jnp.bfloat16)


def draw_key_rows(key, part):
    key = jax.random.fold_in(key, 12)
    return jnp.clip(jax.random.normal(key, (TOKENS, ATT), jnp.float32), -6.0, 6.0).astype(jnp.bfloat16)


def draw_lengths(key, part):
    key = jax.random.fold_in(key, 13)
    first, second = jax.random.split(key)
    base = jax.random.randint(first, (N_DP,), IMAGE // 4, IMAGE + 1)
    chosen = jax.random.randint(second, (), 0, N_DP)
    return jnp.where(jnp.arange(N_DP) == chosen, IMAGE, base).astype(jnp.int32)


def steps_of(key, extent, shards, smallest, high):
    def one(axis_at, blocks):
        draws = jax.random.uniform(jax.random.fold_in(jax.random.fold_in(key, 6), axis_at), (blocks,), jnp.float32, smallest / len(shards), high / len(shards))
        return jnp.repeat(jnp.exp(draws), extent[axis_at] // blocks).reshape((-1,) + (1,) * (len(extent) - axis_at - 1))

    factor_of = one(*shards[0])
    for cut in shards[1:]:
        factor_of = factor_of * one(*cut)
    return factor_of


def normal_values(own_key, shape, scale, limit, cuts=(), held_as=jnp.bfloat16):
    drawn = scale * jax.random.normal(own_key, shape, jnp.float32)
    if cuts:
        drawn = drawn * steps_of(own_key, shape, cuts, -0.22, 0.18)
    return jnp.clip(drawn, -limit, limit).astype(held_as)


def setup_inputs(seed: int = 0) -> dict:
    streams_of = jax.random.split(jax.random.key(seed), 8)
    return {
        "query_rows": draw_query_rows(jax.random.fold_in(streams_of[7], 71), 0),
        "key_rows": draw_key_rows(jax.random.fold_in(streams_of[7], 71), 0),
        "value_rows": normal_values(streams_of[2], (TOKENS, ATT), 1.0, 6.0, ((0, 256),)),
        "d_caption": normal_values(streams_of[3], (CAP_ALL, ATT), 1.0, 6.0, ((0, 256),)),
        "d_image": normal_values(streams_of[4], (IMG_ALL, OUT), 1.0, 6.0, ((0, 256),)),
        "proj_weight": normal_values(streams_of[5], (ATT, OUT), ATT ** -0.5, 0.15625, ((0, 256),)),
        "lengths": draw_lengths(jax.random.fold_in(streams_of[7], 71), 0),
    }


def token_valid(positions, length):
    per_device = CAP_DEV + IMG_DEV
    block = positions // per_device
    offset = positions % per_device
    image_index = block * IMG_DEV + offset - CAP_DEV
    return jnp.logical_or(offset < CAP_DEV, image_index < length)


def one_sequence(total, inputs):
    queries, keyset, values, caption_grad, image_grad, length, proj_weight = inputs
    scale = HD ** -0.5
    valid = token_valid(jnp.arange(SEQ_LEN, dtype=jnp.int32), length)
    image_do = jnp.dot(image_grad, proj_weight.T, preferred_element_type=jnp.float32).astype(jnp.bfloat16)
    grad_out = jnp.concatenate([caption_grad.reshape(N_SEQ, CAP_DEV, ATT), image_do.reshape(N_SEQ, IMG_DEV, ATT)], axis=1).reshape(SEQ_LEN, ATT)
    grad_out = jnp.where(valid[:, None], grad_out, jnp.zeros_like(grad_out))
    q3 = queries.reshape(SEQ_LEN, HEADS, HD).astype(jnp.float32)
    k3 = keyset.reshape(SEQ_LEN, HEADS, HD).astype(jnp.float32)
    v3 = values.reshape(SEQ_LEN, HEADS, HD).astype(jnp.float32)
    g3 = grad_out.reshape(SEQ_LEN, HEADS, HD).astype(jnp.float32)
    scores = jnp.einsum('qhd,khd->hqk', q3, k3) * scale
    scores = jnp.where(valid[None, None, :], scores, -jnp.inf)
    top = jnp.max(scores, axis=-1, keepdims=True)
    expo = jnp.exp(scores - top)
    probs = expo / jnp.sum(expo, axis=-1, keepdims=True)
    probs_low = probs.astype(jnp.bfloat16).astype(jnp.float32)
    attn_out = jnp.einsum('hqk,khd->qhd', probs_low, v3).astype(jnp.bfloat16)
    outs_img = attn_out.reshape(N_SEQ, CAP_DEV + IMG_DEV, ATT)[:, CAP_DEV:, :].reshape(IMAGE, ATT)
    valid_img = valid.reshape(N_SEQ, CAP_DEV + IMG_DEV)[:, CAP_DEV:].reshape(IMAGE)
    outs_img = jnp.where(valid_img[:, None], outs_img, jnp.zeros_like(outs_img))
    total = total + jnp.dot(outs_img.T, image_grad, preferred_element_type=jnp.float32)
    delta = jnp.sum(g3 * attn_out.astype(jnp.float32), axis=-1)
    dprob = jnp.einsum('qhd,khd->hqk', g3, v3)
    dscore = (probs * (dprob - delta.T[:, :, None])).astype(jnp.bfloat16).astype(jnp.float32)
    grad_q = (jnp.einsum('hqk,khd->qhd', dscore, k3) * scale).astype(jnp.bfloat16).reshape(SEQ_LEN, ATT)
    ds4 = dscore.reshape(HEADS, N_SEQ, CAP_DEV + IMG_DEV, SEQ_LEN)
    pb4 = probs_low.reshape(HEADS, N_SEQ, CAP_DEV + IMG_DEV, SEQ_LEN)
    q4 = q3.reshape(N_SEQ, CAP_DEV + IMG_DEV, HEADS, HD)
    g4 = g3.reshape(N_SEQ, CAP_DEV + IMG_DEV, HEADS, HD)
    part_k = (jnp.einsum('hsqk,sqhd->skhd', ds4, q4) * scale).astype(jnp.bfloat16).astype(jnp.float32)
    part_v = jnp.einsum('hsqk,sqhd->skhd', pb4, g4).astype(jnp.bfloat16).astype(jnp.float32)
    grad_k = jnp.sum(part_k, axis=0).astype(jnp.bfloat16).reshape(SEQ_LEN, ATT)
    grad_v = jnp.sum(part_v, axis=0).astype(jnp.bfloat16).reshape(SEQ_LEN, ATT)
    return total, (grad_q, grad_k, grad_v)


def reference(query_rows, key_rows, value_rows, d_caption, d_image, proj_weight, lengths):
    def step(total, inputs):
        return one_sequence(total, inputs + (proj_weight,))

    inputs = (query_rows.reshape(N_DP, SEQ_LEN, ATT), key_rows.reshape(N_DP, SEQ_LEN, ATT),
              value_rows.reshape(N_DP, SEQ_LEN, ATT), d_caption.reshape(N_DP, CAPTION, ATT),
              d_image.reshape(N_DP, IMAGE, OUT), lengths.astype(jnp.int32))
    total, grads = lax.scan(step, jnp.zeros((ATT, OUT), jnp.float32), inputs)
    grad_q, grad_k, grad_v = grads
    return grad_q.reshape(TOKENS, ATT), grad_k.reshape(TOKENS, ATT), grad_v.reshape(TOKENS, ATT), total
```

```python
import jax
import jax.numpy as jnp
from jax import lax
from jax.experimental import pallas as pl
from jax.experimental.pallas import tpu as pltpu
from jax.sharding import PartitionSpec as P

MESH = pl.DeviceIdType.MESH
F32, BF = jnp.float32, jnp.bfloat16
SCALE = 128 ** (-0.5)
LOG2E = 1.4426950408889634
NEG = -1e30
NT = (((1,), (1,)), ((), ()))
TT = (((0,), (0,)), ((), ()))
NN = (((1,), (0,)), ((), ()))


def dot(a, b, dims):
    return lax.dot_general(a, b, dims, preferred_element_type=F32)


def device(x, y, z, c):
    return ((x * 4 + z // 2) * 2 + c, (z % 2) * 4 + y)


def select_rows(half):
    row = lax.broadcasted_iota(jnp.int32, (256, 384), 0)
    col = lax.broadcasted_iota(jnp.int32, (256, 384), 1)
    place, z = row % 32, row // 32
    r, source = place % 8, place // 8
    feature = 48 * ((z // 2) * 2 + half) + 6 * ((z % 2) * 4 + source) + r
    return jnp.where((feature == col) & (r < 6), 1.0, 0.0).astype(BF)


def kernel(
    len_ref, q_ref, k_ref, v_ref, cap_ref, img_ref, w_ref,
    gq_ref, gk_ref, gv_ref, gp_ref,
    kbuf, vbuf, qbuf, dbuf, cbuf, wsend, abuf, wbuf,
    bias, pbuf, plbuf, dsbuf, atbuf, dobuf,
    esend, erecv, gacc, dsend, drecv, csend, crecv, asend, gslot,
    dkown, dvown, dksend, dvsend, zrk, zrv, dqb, dkb, dvb,
    ssem, rsem, lsem,
):
    dp, seq = lax.axis_index("dp"), lax.axis_index("seq")
    c, x = dp % 2, dp // 8
    y, zl = seq % 4, seq // 4
    z = ((dp // 2) % 4) * 2 + zl
    length = len_ref[0]
    here = lambda yy: device(x, yy, z, c)
    mate_z = device(x, y, z + 1 - 2 * zl, c)
    mate_c = device(x, y, z, 1 - c)
    on_diagonal = x == y
    count = [0]
    pending = []

    def slots(n):
        count[0] += n
        return count[0] - n

    def send(src, dst, to, ssl, rsl=None):
        cp = pltpu.make_async_remote_copy(
            src_ref=src, dst_ref=dst, send_sem=ssem.at[ssl], recv_sem=rsem.at[ssl if rsl is None else rsl],
            device_id=to, device_id_type=MESH,
        )
        cp.start()
        pending.append(cp)
        return cp

    def cols(index, width):
        return pl.ds(pl.multiple_of(index * width, 128), width)

    nlocal = [0]

    def local(src, dst):
        cp = pltpu.make_async_copy(src, dst, lsem.at[nlocal[0]])
        nlocal[0] += 1
        cp.start()
        return cp

    own_k = local(k_ref.at[:, cols(y, 384)], kbuf.at[0, y])
    own_v = local(v_ref.at[:, cols(y, 384)], vbuf.at[0, y])
    own_q = local(q_ref.at[:, cols(y, 384)], qbuf.at[y])
    own_d = local(img_ref, dbuf.at[y, pl.ds(16, 112)])
    own_c = local(cap_ref.at[:, cols(y, 384)], cbuf.at[y])

    w = w_ref[...].astype(F32)
    w = jnp.concatenate([w, jnp.zeros((10, 1536), F32)], axis=0).astype(BF)
    for j in range(4):
        wsend[j] = w[:, j * 384:(j + 1) * 384]
    dbuf[:, 0:16, :] = jnp.zeros((4, 16, 1536), BF)

    barrier = pltpu.get_barrier_semaphore()

    def greet(to):
        pl.semaphore_signal(barrier, inc=1, device_id=to, device_id_type=MESH)

    for i in range(1, 4):
        greet(here((y + i) % 4))
        greet(device((x + i) % 4, y, z, c))
    for i in range(1, 8):
        greet(device(x, y, (z + i) % 8, c))
    greet(mate_c)
    for j in range(4):
        @pl.when(jnp.logical_not(on_diagonal & (x == j)))
        def _():
            greet(device(j, x, z, c))

        @pl.when(jnp.logical_not(on_diagonal & (y == j)))
        def _():
            greet(device(y, j, z, c))
    pl.semaphore_wait(barrier, 22 - 2 * on_diagonal.astype(jnp.int32))

    kv = []
    base = slots(6)
    for i in range(1, 4):
        p = (y + i) % 4
        a = send(k_ref.at[:, cols(p, 384)], kbuf.at[0, y], here(p), base + 2 * i - 2)
        b = send(v_ref.at[:, cols(p, 384)], vbuf.at[0, y], here(p), base + 2 * i - 1)
        kv.append((a, b))
    zbase = slots(8)
    zk = [send(k_ref.at[:, cols(y, 384)], kbuf.at[1, y], mate_z, zbase)]
    zv = [send(v_ref.at[:, cols(y, 384)], vbuf.at[1, y], mate_z, zbase + 1)]

    wa = slots(4)

    def wa_copy(j, to):
        return pltpu.make_async_remote_copy(
            src_ref=wsend.at[j], dst_ref=abuf.at[y], send_sem=ssem.at[wa + j], recv_sem=rsem.at[wa + y],
            device_id=to, device_id_type=MESH,
        )

    def wa_local(j):
        return pltpu.make_async_copy(wsend.at[j], abuf.at[y], lsem.at[7])

    for j in range(4):
        mine = on_diagonal & (x == j)

        @pl.when(mine)
        def _():
            wa_local(j).start()

        @pl.when(jnp.logical_not(mine))
        def _():
            wa_copy(j, device(j, x, z, c)).start()
    for j in range(4):
        mine = on_diagonal & (x == j)

        @pl.when(mine)
        def _():
            wa_local(j).wait()

        @pl.when(jnp.logical_not(mine))
        def _():
            wa_copy(j, device(j, x, z, c)).wait_send()
            pltpu.make_async_remote_copy(
                src_ref=wsend.at[j], dst_ref=abuf.at[j], send_sem=ssem.at[wa + j], recv_sem=rsem.at[wa + j],
                device_id=mate_c, device_id_type=MESH,
            ).wait_recv()
    rows = jnp.concatenate([abuf[j].astype(F32)[0:8] for j in range(4)], axis=0).astype(BF)
    zrows = lambda zz: pl.ds(pl.multiple_of(zz * 32, 32), 32)
    wbuf[c, x, zrows(z), :] = rows
    wc = []
    base = slots(7)
    for i in range(1, 8):
        piece = wbuf.at[c, x, zrows(z)]
        wc.append(send(piece, piece, device(x, y, (z + i) % 8, c), base + i - 1))

    own_k.wait()
    own_v.wait()
    for i in (1, 3, 2):
        p = (y + 4 - i) % 4
        a, b = kv[i - 1]
        a.wait_recv()
        zk.append(send(kbuf.at[0, p], kbuf.at[1, p], mate_z, zbase + 2 * i))
        b.wait_recv()
        zv.append(send(vbuf.at[0, p], vbuf.at[1, p], mate_z, zbase + 2 * i + 1))
    base = slots(9)
    qs, ds, cs = [], [], []
    for i in range(1, 4):
        p = (y + i) % 4
        qs.append(send(q_ref.at[:, cols(p, 384)], qbuf.at[y], here(p), base + i - 1))
    for i in range(1, 4):
        p = (y + i) % 4
        cs.append(send(cap_ref.at[:, cols(p, 384)], cbuf.at[y], here(p), base + 2 + i))
        ds.append(send(img_ref, dbuf.at[y, pl.ds(16, 112)], here(p), base + 5 + i))

    for cp in wc:
        cp.wait_recv()
    wd = []
    base = slots(3)
    for i in range(1, 4):
        wd.append(send(wbuf.at[c, x], wbuf.at[c, x], device((x + i) % 4, y, z, c), base + i - 1))

    ki = lax.broadcasted_iota(jnp.int32, (1024, 256), 0)
    blk = jnp.where(ki < 512, zl, 1 - zl) * 4 + (ki // 128) % 4
    off = ki % 128
    token = blk * 112 + off - 16
    bias[...] = jnp.where((off < 16) | (token < length), 0.0, NEG)

    own_q.wait()
    for cp in qs + zk + zv:
        cp.wait_recv()

    def forward(h):
        lanes = slice(h * 128, (h + 1) * 128)
        kk = kbuf[:, :, :, lanes].reshape(1024, 128)
        vv = vbuf[:, :, :, lanes].reshape(1024, 128)
        for t in range(2):
            qq = qbuf[2 * t:2 * t + 2, :, lanes].reshape(256, 128)
            s = dot(kk, qq, NT) + bias[...]
            top = jnp.max(s, axis=0, keepdims=True)
            e = jnp.exp2((s - top) * (SCALE * LOG2E))
            prob = e * (1.0 / jnp.sum(e, axis=0, keepdims=True))
            low = prob.astype(BF)
            pbuf[h, :, t * 256:(t + 1) * 256] = prob
            plbuf[h, :, t * 256:(t + 1) * 256] = low
            atbuf[h * 128:(h + 1) * 128, t * 256:(t + 1) * 256] = dot(vv, low, TT).astype(BF)

    forward(0)
    for cp in wd:
        cp.wait_recv()
    we = send(wbuf.at[c], wbuf.at[c], mate_c, slots(1))
    forward(1)
    forward(2)

    own_d.wait()
    own_c.wait()
    for cp in ds + cs:
        cp.wait_recv()
    qi = lax.broadcasted_iota(jnp.int32, (384, 512), 1)
    off = qi % 128
    token = (zl * 4 + qi // 128) * 112 + off - 16
    image = (off >= 16) & (token < length)
    at_image = jnp.where(image, atbuf[...].astype(F32), 0.0).astype(BF)

    def project(half):
        padded = dot(select_rows(half), at_image, NN).astype(BF)
        return [dot(padded, dbuf[:, :, j * 384:(j + 1) * 384].reshape(512, 384), NN) for j in range(4)]

    for j, part in enumerate(project(1 - c)):
        esend[j] = part.astype(BF)
    ge = send(esend, erecv, mate_c, slots(1))
    for j, part in enumerate(project(c)):
        gacc[j] = part

    we.wait_recv()
    do_all = jnp.zeros((512, 384), F32)
    for half in range(2):
        padded = jnp.zeros((512, 256), F32)
        for j in range(4):
            padded += dot(dbuf[:, :, j * 384:(j + 1) * 384].reshape(512, 384), wbuf[half, j], NT)
        do_all += dot(padded.astype(BF), select_rows(half), NN)
    ri = lax.broadcasted_iota(jnp.int32, (512, 384), 0)
    token = (zl * 4 + ri // 128) * 112 + ri % 128 - 16
    dobuf[...] = jnp.where(token < length, do_all, 0.0).astype(BF)
    for p in range(4):
        dobuf[p * 128:p * 128 + 16, :] = cbuf[p]

    ge.wait_recv()
    for j in range(4):
        total = gacc[j] + erecv[j].astype(F32)
        gacc[j] = total
        dsend[j] = total.astype(BF)
    base = slots(3)
    gd = []
    for i in range(1, 4):
        xx = (x + i) % 4
        gd.append(send(dsend.at[xx], drecv.at[i - 1], device(xx, y, z, c), base + i - 1))

    ybase = slots(27)
    zrbase = slots(6)
    zsent = []

    def to_rows(src, out, which, h):
        cps = []
        lane = cols(y * 3 + h, 128)
        for i in range(1, 4):
            p = (y + i) % 4
            piece = src.at[h, pl.ds(pl.multiple_of(p * 128, 128), 128)]
            cps.append(send(piece, out.at[:, lane], here(p), ybase + which * 9 + h * 3 + i - 1))
        piece = src.at[h, pl.ds(pl.multiple_of(y * 128, 128), 128)]
        return cps, local(piece, out.at[:, lane])

    nlocal[0] = 8
    results = []

    def backward(h):
        lanes = slice(h * 128, (h + 1) * 128)
        kk = kbuf[:, :, :, lanes].reshape(1024, 128)
        vv = vbuf[:, :, :, lanes].reshape(1024, 128)
        for t in range(2):
            part = slice(t * 256, (t + 1) * 256)
            do = dobuf[part, lanes]
            delta = jnp.sum(do.astype(F32).T * atbuf[lanes, part].astype(F32), axis=0, keepdims=True)
            dsbuf[:, part] = (pbuf[h, :, part] * (dot(vv, do, NT) - delta)).astype(BF)
        dv = dot(plbuf[h], dobuf[:, lanes], NN)
        dvown[h] = dv[0:512]
        dvsend[h] = dv[512:1024].astype(BF)
        dk = dot(dsbuf[...], qbuf[:, :, lanes].reshape(512, 128), NN) * SCALE
        dkown[h] = dk[0:512]
        dksend[h] = dk[512:1024].astype(BF)
        zsent.append((
            send(dksend.at[h], zrk.at[h], mate_z, zrbase + 2 * h),
            send(dvsend.at[h], zrv.at[h], mate_z, zrbase + 2 * h + 1),
        ))
        dqb[h] = (dot(kk, dsbuf[...], TT) * SCALE).T.astype(BF)
        results.append(to_rows(dqb, gq_ref, 0, h))

    def settle(h):
        a, b = zsent[h]
        a.wait_recv()
        dkb[h] = (dkown[h] + zrk[h].astype(F32)).astype(BF)
        results.append(to_rows(dkb, gk_ref, 1, h))
        b.wait_recv()
        dvb[h] = (dvown[h] + zrv[h].astype(F32)).astype(BF)
        results.append(to_rows(dvb, gv_ref, 2, h))

    backward(0)
    for cp in gd:
        cp.wait_recv()
    total = gacc[x] + drecv[0].astype(F32) + drecv[1].astype(F32) + drecv[2].astype(F32)
    gacc[x] = total
    csend[...] = total.astype(BF).reshape(8, 32, 384)
    base = slots(7)
    gc = []
    for i in range(1, 8):
        zz = (z + i) % 8
        gc.append(send(csend.at[zz], crecv.at[i - 1], device(x, y, zz, c), base + i - 1))

    backward(1)
    for cp in gc:
        cp.wait_recv()
    total = gacc[x, zrows(z), :]
    for i in range(7):
        total += crecv[i].astype(F32)
    asend[...] = total
    ga = slots(4)

    def ga_copy(j, to):
        return pltpu.make_async_remote_copy(
            src_ref=asend.at[pl.ds(j * 8, 8)], dst_ref=gslot.at[x], send_sem=ssem.at[ga + j], recv_sem=rsem.at[ga + x],
            device_id=to, device_id_type=MESH,
        )

    def ga_local(j):
        return pltpu.make_async_copy(asend.at[pl.ds(j * 8, 8)], gslot.at[x], lsem.at[6])

    for j in range(4):
        mine = on_diagonal & (y == j)

        @pl.when(mine)
        def _():
            ga_local(j).start()

        @pl.when(jnp.logical_not(mine))
        def _():
            ga_copy(j, device(y, j, z, c)).start()

    backward(2)
    for h in range(3):
        settle(h)
    for j in range(4):
        mine = on_diagonal & (y == j)

        @pl.when(mine)
        def _():
            ga_local(j).wait()

        @pl.when(jnp.logical_not(mine))
        def _():
            ga_copy(j, device(y, j, z, c)).wait_send()
            pltpu.make_async_remote_copy(
                src_ref=asend.at[pl.ds(j * 8, 8)], dst_ref=gslot.at[j], send_sem=ssem.at[ga + j],
                recv_sem=rsem.at[ga + j], device_id=mate_c, device_id_type=MESH,
            ).wait_recv()
    for j in range(4):
        gp_ref[:, j * 384:(j + 1) * 384] = gslot[j][0:6]
    for cps, own in results:
        for cp in cps:
            cp.wait_recv()
        own.wait()
    for cp in pending:
        cp.wait_send()
    assert count[0] <= 100 and nlocal[0] <= 20


def shards(query_rows, key_rows, value_rows, d_caption, d_image, proj_weight, lengths):
    rows = jax.ShapeDtypeStruct((128, 1536), BF)
    hbm = pl.BlockSpec(memory_space=pl.ANY)
    vmem = pl.BlockSpec(memory_space=pltpu.VMEM)
    scratch = [
        pltpu.VMEM(shape, dtype)
        for shape, dtype in (
            ((2, 4, 128, 384), BF), ((2, 4, 128, 384), BF), ((4, 128, 384), BF), ((4, 128, 1536), BF),
            ((4, 16, 384), BF), ((4, 16, 384), BF), ((4, 16, 384), BF), ((2, 4, 256, 384), BF),
            ((1024, 256), F32), ((3, 1024, 512), F32), ((3, 1024, 512), BF), ((1024, 512), BF),
            ((384, 512), BF), ((512, 384), BF),
            ((4, 256, 384), BF), ((4, 256, 384), BF), ((4, 256, 384), F32), ((4, 256, 384), BF),
            ((3, 256, 384), BF), ((8, 32, 384), BF), ((7, 32, 384), BF), ((32, 384), F32), ((4, 8, 384), F32),
            ((3, 512, 128), F32), ((3, 512, 128), F32), ((3, 512, 128), BF), ((3, 512, 128), BF),
            ((3, 512, 128), BF), ((3, 512, 128), BF), ((3, 512, 128), BF), ((3, 512, 128), BF), ((3, 512, 128), BF),
        )
    ]
    return pl.pallas_call(
        kernel,
        out_shape=(rows, rows, rows, jax.ShapeDtypeStruct((6, 1536), F32)),
        in_specs=[pl.BlockSpec(memory_space=pltpu.SMEM), hbm, hbm, hbm, hbm, hbm, vmem],
        out_specs=(hbm, hbm, hbm, vmem),
        scratch_shapes=scratch + [
            pltpu.SemaphoreType.DMA((100,)), pltpu.SemaphoreType.DMA((100,)), pltpu.SemaphoreType.DMA((20,)),
        ],
        compiler_params=pltpu.CompilerParams(
            collective_id=0, has_side_effects=True, vmem_limit_bytes=56 * 2**20
        ),
        name="joint_attention_backward",
    )(lengths, query_rows, key_rows, value_rows, d_caption, d_image, proj_weight)


def solution(mesh):
    placed = P(("dp", "seq"), None)
    return jax.shard_map(
        shards,
        mesh=mesh,
        in_specs=(placed,) * 6 + (P("dp"),),
        out_specs=(placed,) * 4,
        check_vma=False,
    )
```

```python
import jax
import jax.numpy as jnp
from jax import lax
from jax.experimental import pallas as pl
from jax.experimental.pallas import tpu as pltpu
from jax.sharding import PartitionSpec as P

MESH = pl.DeviceIdType.MESH
F32, BF = jnp.float32, jnp.bfloat16
SCALE = 128 ** (-0.5)
EXP_SCALE = SCALE * 1.4426950408889634
NEG = -1e30
NT = (((1,), (1,)), ((), ()))
TT = (((0,), (0,)), ((), ()))
NN = (((1,), (0,)), ((), ()))
SEMS, LOCALS = 180, 32


def dot(a, b, dims):
    return lax.dot_general(a, b, dims, preferred_element_type=F32)


def device(x, y, z, c):
    return ((x * 4 + z // 2) * 2 + c, (z % 2) * 4 + y)


def select(rows, cols, pick):
    r = lax.broadcasted_iota(jnp.int32, (rows, cols), 0)
    c = lax.broadcasted_iota(jnp.int32, (rows, cols), 1)
    return jnp.where(pick(r, c), 1.0, 0.0).astype(BF)


def kernel(
    len_ref, q_ref, k_ref, v_ref, cap_ref, img_ref, w_ref,
    gq_ref, gk_ref, gv_ref, gp_ref,
    kvb, qb, dbuf, cbuf, wsend, abuf, wz, wbuf,
    bias, pbuf, lowbuf, dsbuf, p2buf, low2buf, ds2buf, atbuf, dob, lse, delta,
    esend, erecv, gacc, dsend, drecv, csend, crecv, asend, gslot,
    dkown, dvown, dqb, dkb, dvb,
    ssem, rsem, lsem,
):
    dp, seq = lax.axis_index("dp"), lax.axis_index("seq")
    c, x = dp % 2, dp // 8
    y, zl = seq % 4, seq // 4
    z = ((dp // 2) % 4) * 2 + zl
    length = len_ref[0]
    mate_z = device(x, y, z + 1 - 2 * zl, c)
    mate_c = device(x, y, z, 1 - c)
    on_diagonal = x == y
    count = [0, 0]
    pending = []

    def at_y(yy):
        return device(x, yy, z, c)

    def slots(n):
        count[0] += n
        return count[0] - n

    def send(src, dst, to, slot):
        cp = pltpu.make_async_remote_copy(
            src_ref=src, dst_ref=dst, send_sem=ssem.at[slot], recv_sem=rsem.at[slot],
            device_id=to, device_id_type=MESH,
        )
        cp.start()
        pending.append(cp)
        return cp

    def local(src, dst):
        cp = pltpu.make_async_copy(src, dst, lsem.at[count[1]])
        count[1] += 1
        cp.start()
        return cp

    def cols(index, width):
        return pl.ds(pl.multiple_of(index * width, 128), width)

    def rows(index, height):
        return pl.ds(pl.multiple_of(index * height, height), height)

    barrier = pltpu.get_barrier_semaphore()

    def greet(to):
        pl.semaphore_signal(barrier, inc=1, device_id=to, device_id_type=MESH)

    for i in range(1, 4):
        greet(at_y((y + i) % 4))
        greet(device((x + i) % 4, y, z, c))
    for i in range(1, 8):
        greet(device(x, y, (z + i) % 8, c))
    greet(mate_c)
    for j in range(4):
        @pl.when(jnp.logical_not(on_diagonal & (x == j)))
        def _():
            greet(device(j, x, z, c))

        @pl.when(jnp.logical_not(on_diagonal & (y == j)))
        def _():
            greet(device(y, j, z, c))
    own = []
    for h in range(3):
        lane = cols(y * 3 + h, 128)
        own.append(local(k_ref.at[:, lane], kvb.at[h, 0, y, 0]))
        own.append(local(v_ref.at[:, lane], kvb.at[h, 0, y, 1]))
        own.append(local(q_ref.at[:, lane], qb.at[h, 0, y]))
    own.append(local(img_ref, dbuf.at[y, pl.ds(16, 112)]))
    own.append(local(cap_ref.at[:, cols(y, 384)], cbuf.at[y]))

    w = jnp.concatenate([w_ref[...].astype(F32), jnp.zeros((10, 1536), F32)], axis=0).astype(BF)
    for j in range(4):
        wsend[j] = w[:, j * 384:(j + 1) * 384]
    dbuf[:, 0:16, :] = jnp.zeros((4, 16, 1536), BF)

    ki = lax.broadcasted_iota(jnp.int32, (1024, 256), 0)
    blk = jnp.where(ki < 512, zl, 1 - zl) * 4 + (ki // 128) % 4
    off = ki % 128
    bias[...] = jnp.where((off < 16) | (blk * 112 + off - 16 < length), 0.0, NEG)
    for cp in own:
        cp.wait()

    pl.semaphore_wait(barrier, 22 - 2 * on_diagonal.astype(jnp.int32))

    wa = slots(4)

    def wa_copy(j, to):
        return pltpu.make_async_remote_copy(
            src_ref=wsend.at[j], dst_ref=abuf.at[y], send_sem=ssem.at[wa + j], recv_sem=rsem.at[wa + y],
            device_id=to, device_id_type=MESH,
        )

    def wa_local(j):
        return pltpu.make_async_copy(wsend.at[j], abuf.at[y], lsem.at[LOCALS - 1])

    for j in range(4):
        mine = on_diagonal & (x == j)

        @pl.when(mine)
        def _():
            wa_local(j).start()

        @pl.when(jnp.logical_not(mine))
        def _():
            wa_copy(j, device(j, x, z, c)).start()

    ybase = slots(27)
    came = [[] for _ in range(3)]

    def exchange(h):
        for i in (1, 3, 2):
            p = (y + i) % 4
            lane = cols(p * 3 + h, 128)
            slot = ybase + 9 * h + 3 * (i - 1)
            came[h].append((
                (y + 4 - i) % 4, i,
                send(k_ref.at[:, lane], kvb.at[h, 0, y, 0], at_y(p), slot),
                send(v_ref.at[:, lane], kvb.at[h, 0, y, 1], at_y(p), slot + 1),
                send(q_ref.at[:, lane], qb.at[h, 0, y], at_y(p), slot + 2),
            ))

    zbase = slots(24)
    far_kv, far_q = [[] for _ in range(3)], [[] for _ in range(3)]

    def pass_kv(h, p, i):
        far_kv[h].append(send(kvb.at[h, 0, p], kvb.at[h, 1, p], mate_z, zbase + 4 * h + i))

    def pass_q(h, p, i):
        far_q[h].append(send(qb.at[h, 0, p], qb.at[h, 1, p], mate_z, zbase + 12 + 4 * h + i))

    exchange(0)
    for h in range(3):
        pass_kv(h, y, 0)
    exchange(1)
    exchange(2)

    dbase = slots(4)
    mine_d = dbuf.at[y, pl.ds(16, 112)]
    ds = [send(mine_d, mine_d, at_y((y + 1) % 4), dbase), send(mine_d, mine_d, at_y((y + 3) % 4), dbase + 1)]
    capbase = slots(3)
    cs = [
        send(cap_ref.at[:, cols((y + i) % 4, 384)], cbuf.at[y], at_y((y + i) % 4), capbase + i - 1)
        for i in range(1, 4)
    ]
    for j in range(4):
        mine = on_diagonal & (x == j)

        @pl.when(mine)
        def _():
            wa_local(j).wait()

        @pl.when(jnp.logical_not(mine))
        def _():
            wa_copy(j, device(j, x, z, c)).wait_send()
            pltpu.make_async_remote_copy(
                src_ref=wsend.at[j], dst_ref=abuf.at[j], send_sem=ssem.at[wa + j], recv_sem=rsem.at[wa + j],
                device_id=mate_c, device_id_type=MESH,
            ).wait_recv()
    padded = jnp.concatenate([abuf[j].astype(F32)[0:8] for j in range(4)], axis=0).astype(BF)
    squeeze = select(32, 32, lambda r, k: (k % 8 < 6) & (r == k // 8 * 6 + k % 8))
    wz[z] = dot(squeeze, padded, NN).astype(BF)
    base = slots(7)
    wc = [send(wz.at[z], wz.at[z], device(x, y, (z + i) % 8, c), base + i - 1) for i in range(1, 8)]

    def pass_on(h):
        for p, i, a, b, _ in came[h]:
            a.wait_recv()
            b.wait_recv()
            pass_kv(h, p, i)

    pass_on(0)
    pass_on(1)
    for cp in wc:
        cp.wait_recv()
    wbuf[c, x] = jnp.concatenate([wz[i].astype(F32)[0:24] for i in range(8)], axis=0).astype(BF)
    base = slots(4)
    wd = [
        send(wbuf.at[c, x], wbuf.at[c, x], device((x + 1) % 4, y, z, c), base),
        send(wbuf.at[c, x], wbuf.at[c, x], device((x + 3) % 4, y, z, c), base + 1),
    ]
    pass_on(2)
    for h in range(3):
        pass_q(h, y, 0)
        for p, i, _, _, q in came[h]:
            q.wait_recv()
            pass_q(h, p, i)

    def whole(buf, h, which):
        return buf[h, :, :, which].reshape(1024, 128)

    def forward(h):
        for cp in far_kv[h]:
            cp.wait_recv()
        kk, vv = whole(kvb, h, 0), whole(kvb, h, 1)
        for t in range(2):
            part = slice(t * 256, (t + 1) * 256)
            qq = qb[h, 0, 2 * t:2 * t + 2].reshape(256, 128)
            s = dot(kk, qq, NT) + bias[...]
            top = jnp.max(s, axis=0, keepdims=True)
            e = jnp.exp2((s - top) * EXP_SCALE)
            total = jnp.sum(e, axis=0, keepdims=True)
            prob = e * (1.0 / total)
            low = prob.astype(BF)
            pbuf[h, :, part] = prob
            lowbuf[h, :, part] = low
            atbuf[h * 128:(h + 1) * 128, part] = dot(vv, low, TT).astype(BF)
            lse[0, h:h + 1, part] = top * EXP_SCALE + jnp.log2(total)

    forward(0)
    for cp in wd:
        cp.wait_recv()
    low_half = wbuf.at[c, (x + 3) % 4, pl.ds(0, 96)]
    high_half = wbuf.at[c, (x + 1) % 4, pl.ds(96, 96)]
    wd2 = [
        send(low_half, low_half, device((x + 1) % 4, y, z, c), base + 2),
        send(high_half, high_half, device((x + 3) % 4, y, z, c), base + 3),
    ]
    forward(1)
    ds[0].wait_recv()
    piece = dbuf.at[(y + 3) % 4, pl.ds(16, 64)]
    ds.append(send(piece, piece, at_y((y + 1) % 4), dbase + 2))
    ds[1].wait_recv()
    piece = dbuf.at[(y + 1) % 4, pl.ds(80, 48)]
    ds.append(send(piece, piece, at_y((y + 3) % 4), dbase + 3))

    for cp in wd2:
        cp.wait_recv()
    we = send(wbuf.at[c], wbuf.at[c], mate_c, slots(1))
    forward(2)
    stat = slots(2)
    far_lse = send(lse.at[0], lse.at[1], mate_z, stat)

    qi = lax.broadcasted_iota(jnp.int32, (384, 512), 1)
    off = qi % 128
    token = (zl * 4 + qi // 128) * 112 + off - 16
    at_image = jnp.where((off >= 16) & (token < length), atbuf[...].astype(F32), 0.0)
    blocks = [at_image[i * 48:(i + 1) * 48] for i in range(8)]
    ones = jnp.zeros((48, 512), jnp.int32) + c
    first = jnp.concatenate([jnp.where(ones == 0, blocks[2 * i + 1], blocks[2 * i]) for i in range(4)], axis=0).astype(BF)
    second = jnp.concatenate([jnp.where(ones == 0, blocks[2 * i], blocks[2 * i + 1]) for i in range(4)], axis=0).astype(BF)
    for cp in cs:
        cp.wait_recv()
    for cp in ds[2:]:
        cp.wait_recv()

    def image_cols(j):
        return dbuf[:, :, j * 384:(j + 1) * 384].reshape(512, 384)

    for j in range(4):
        esend[j] = dot(first, image_cols(j), NN).astype(BF)
    ge = send(esend, erecv, mate_c, slots(1))

    for j in range(4):
        gacc[j] = dot(second, image_cols(j), NN)

    we.wait_recv()
    do_all = jnp.zeros((512, 384), F32)
    for j in range(4):
        wj = jnp.concatenate(
            [wbuf[i % 2, j, i // 2 * 48:(i // 2 + 1) * 48] for i in range(8)], axis=0
        )
        do_all += dot(image_cols(j), wj, NT)
    ri = lax.broadcasted_iota(jnp.int32, (512, 384), 0)
    token = (zl * 4 + ri // 128) * 112 + ri % 128 - 16
    do_all = jnp.where(token < length, do_all, 0.0).astype(BF)
    dobase = slots(3)
    far_do = []
    for h in range(3):
        lanes = slice(h * 128, (h + 1) * 128)
        for p in range(4):
            dob[h, 0, p, 0:16] = cbuf[p, :, lanes]
            dob[h, 0, p, 16:128] = do_all[p * 128 + 16:(p + 1) * 128, lanes]
        far_do.append(send(dob.at[h, 0], dob.at[h, 1], mate_z, dobase + h))
        for t in range(2):
            part = slice(t * 256, (t + 1) * 256)
            do = dob[h, 0, 2 * t:2 * t + 2].reshape(256, 128)
            delta[0, h:h + 1, part] = jnp.sum(
                do.astype(F32).T * atbuf[lanes, part].astype(F32), axis=0, keepdims=True
            )
    far_delta = send(delta.at[0], delta.at[1], mate_z, stat + 1)

    rbase = slots(27)
    results = []

    def to_rows(src, out, which, h):
        lane = cols(y * 3 + h, 128)
        for i in (1, 3, 2):
            p = (y + i) % 4
            results.append(send(src.at[h, rows(p, 128)], out.at[:, lane], at_y(p), rbase + which * 9 + h * 3 + i - 1))
        finals.append(local(src.at[h, rows(y, 128)], out.at[:, lane]))

    finals = []

    def backward(h):
        kk, vv = whole(kvb, h, 0), whole(kvb, h, 1)
        for t in range(2):
            part = slice(t * 256, (t + 1) * 256)
            do = dob[h, 0, 2 * t:2 * t + 2].reshape(256, 128)
            dsbuf[:, part] = (pbuf[h, :, part] * (dot(vv, do, NT) - delta[0, h:h + 1, part])).astype(BF)
        dqb[h] = (dot(kk, dsbuf[...], TT) * SCALE).T.astype(BF)
        to_rows(dqb, gq_ref, 0, h)
        dvown[h] = dot(lowbuf[h, 0:512], dob[h, 0].reshape(512, 128), NN)
        dkown[h] = dot(dsbuf[0:512], qb[h, 0].reshape(512, 128), NN)

    def far_probs(h):
        for cp in far_q[h]:
            cp.wait_recv()
        kk = kvb[h, 0, :, 0].reshape(512, 128)
        for t in range(2):
            part = slice(t * 256, (t + 1) * 256)
            s = dot(kk, qb[h, 1, 2 * t:2 * t + 2].reshape(256, 128), NT) + bias[0:512]
            prob = jnp.exp2(s * EXP_SCALE - lse[1, h:h + 1, part])
            p2buf[h, :, part] = prob
            low2buf[h, :, part] = prob.astype(BF)

    def far_backward(h):
        far_do[h].wait_recv()
        vv = kvb[h, 0, :, 1].reshape(512, 128)
        for t in range(2):
            part = slice(t * 256, (t + 1) * 256)
            do = dob[h, 1, 2 * t:2 * t + 2].reshape(256, 128)
            ds2buf[:, part] = (p2buf[h, :, part] * (dot(vv, do, NT) - delta[1, h:h + 1, part])).astype(BF)
        dkb[h] = ((dkown[h] + dot(ds2buf[...], qb[h, 1].reshape(512, 128), NN)) * SCALE).astype(BF)
        to_rows(dkb, gk_ref, 1, h)
        dvb[h] = (dvown[h] + dot(low2buf[h], dob[h, 1].reshape(512, 128), NN)).astype(BF)
        to_rows(dvb, gv_ref, 2, h)

    ge.wait_recv()
    for j in range(4):
        total = gacc[j] + erecv[j].astype(F32)
        gacc[j] = total
        dsend[j] = total.astype(BF)
    base = slots(3)
    gd = []
    for i in range(1, 4):
        xx = (x + i) % 4
        gd.append(send(dsend.at[xx], drecv.at[i - 1], device(xx, y, z, c), base + i - 1))
    backward(0)
    backward(1)
    backward(2)
    far_lse.wait_recv()
    for h in range(3):
        far_probs(h)
    far_delta.wait_recv()
    far_backward(0)
    far_backward(1)

    for cp in gd:
        cp.wait_recv()
    total = gacc[x] + drecv[0].astype(F32) + drecv[1].astype(F32) + drecv[2].astype(F32)
    spread = select(256, 192, lambda r, k: (r % 8 < 6) & (k == r // 8 * 6 + r % 8))
    csend[...] = dot(spread, total.astype(BF), NN).astype(BF).reshape(8, 32, 384)
    base = slots(7)
    gc = []
    for i in range(1, 8):
        zz = (z + i) % 8
        gc.append(send(csend.at[zz], crecv.at[i - 1], device(x, y, zz, c), base + i - 1))
    far_backward(2)

    total = csend[z].astype(F32)
    for i in range(7):
        gc[i].wait_recv()
        total += crecv[i].astype(F32)
    asend[...] = total
    ga = slots(4)

    def ga_copy(j, to):
        return pltpu.make_async_remote_copy(
            src_ref=asend.at[pl.ds(j * 8, 8)], dst_ref=gslot.at[x], send_sem=ssem.at[ga + j], recv_sem=rsem.at[ga + x],
            device_id=to, device_id_type=MESH,
        )

    def ga_local(j):
        return pltpu.make_async_copy(asend.at[pl.ds(j * 8, 8)], gslot.at[x], lsem.at[LOCALS - 2])

    for j in range(4):
        mine = on_diagonal & (y == j)

        @pl.when(mine)
        def _():
            ga_local(j).start()

        @pl.when(jnp.logical_not(mine))
        def _():
            ga_copy(j, device(y, j, z, c)).start()

    for j in range(4):
        mine = on_diagonal & (y == j)

        @pl.when(mine)
        def _():
            ga_local(j).wait()

        @pl.when(jnp.logical_not(mine))
        def _():
            ga_copy(j, device(y, j, z, c)).wait_send()
            pltpu.make_async_remote_copy(
                src_ref=asend.at[pl.ds(j * 8, 8)], dst_ref=gslot.at[j], send_sem=ssem.at[ga + j],
                recv_sem=rsem.at[ga + j], device_id=mate_c, device_id_type=MESH,
            ).wait_recv()
    for j in range(4):
        gp_ref[:, j * 384:(j + 1) * 384] = gslot[j][0:6]
    for cp in results:
        cp.wait_recv()
    for cp in finals:
        cp.wait()
    for cp in pending:
        cp.wait_send()
    assert count[0] <= SEMS and count[1] <= LOCALS - 2


def copy_out(*refs):
    half = len(refs) // 2
    for src, dst in zip(refs[:half], refs[half:]):
        dst[...] = src[...]


def shards(query_rows, key_rows, value_rows, d_caption, d_image, proj_weight, lengths):
    block = jax.ShapeDtypeStruct((128, 1536), BF)
    outs = (block, block, block, jax.ShapeDtypeStruct((6, 1536), F32))
    hbm = pl.BlockSpec(memory_space=pl.ANY)
    vmem = pl.BlockSpec(memory_space=pltpu.VMEM)
    scratch = [
        pltpu.VMEM(shape, dtype)
        for shape, dtype in (
            ((3, 2, 4, 2, 128, 128), BF), ((3, 2, 4, 128, 128), BF), ((4, 128, 1536), BF), ((4, 16, 384), BF),
            ((4, 16, 384), BF), ((4, 16, 384), BF), ((8, 32, 384), BF), ((2, 4, 192, 384), BF),
            ((1024, 256), F32), ((3, 1024, 512), F32), ((3, 1024, 512), BF), ((1024, 512), BF),
            ((3, 512, 512), F32), ((3, 512, 512), BF), ((512, 512), BF),
            ((384, 512), BF), ((3, 2, 4, 128, 128), BF), ((2, 8, 512), F32), ((2, 8, 512), F32),
            ((4, 192, 384), BF), ((4, 192, 384), BF), ((4, 192, 384), F32), ((4, 192, 384), BF),
            ((3, 192, 384), BF), ((8, 32, 384), BF), ((7, 32, 384), BF), ((32, 384), F32), ((4, 8, 384), F32),
            ((3, 512, 128), F32), ((3, 512, 128), F32),
            ((3, 512, 128), BF), ((3, 512, 128), BF), ((3, 512, 128), BF),
        )
    ]
    results = pl.pallas_call(
        kernel,
        out_shape=outs,
        in_specs=[pl.BlockSpec(memory_space=pltpu.SMEM), hbm, hbm, hbm, hbm, hbm, vmem],
        out_specs=(hbm, hbm, hbm, vmem),
        scratch_shapes=scratch + [
            pltpu.SemaphoreType.DMA((SEMS,)), pltpu.SemaphoreType.DMA((SEMS,)), pltpu.SemaphoreType.DMA((LOCALS,)),
        ],
        compiler_params=pltpu.CompilerParams(
            collective_id=0, has_side_effects=True, vmem_limit_bytes=56 * 2**20
        ),
        name="joint_attention_backward",
    )(lengths, query_rows, key_rows, value_rows, d_caption, d_image, proj_weight)
    return pl.pallas_call(
        copy_out,
        out_shape=outs,
        in_specs=[vmem] * 4,
        out_specs=(vmem,) * 4,
        name="copy_out",
    )(*results)


def solution(mesh):
    placed = P(("dp", "seq"), None)
    return jax.shard_map(
        shards,
        mesh=mesh,
        in_specs=(placed,) * 6 + (P("dp"),),
        out_specs=(placed,) * 4,
        check_vma=False,
    )
```

```python
import jax
import jax.numpy as jnp
from jax import lax
from jax.experimental import pallas as pl
from jax.experimental.pallas import tpu as pltpu
from jax.sharding import PartitionSpec as P

MESH = pl.DeviceIdType.MESH
F32, BF = jnp.float32, jnp.bfloat16
SCALE = 128 ** (-0.5)
EXP_SCALE = SCALE * 1.4426950408889634
NEG = -1e30
NT = (((1,), (1,)), ((), ()))
TT = (((0,), (0,)), ((), ()))
NN = (((1,), (0,)), ((), ()))
SEMS, LOCALS = 40, 7


def dot(a, b, dims):
    return lax.dot_general(a, b, dims, preferred_element_type=F32)


def device(x, y, z, c):
    return ((x * 4 + z // 2) * 2 + c, (z % 2) * 4 + y)


def select(rows, cols, pick):
    r = lax.broadcasted_iota(jnp.int32, (rows, cols), 0)
    c = lax.broadcasted_iota(jnp.int32, (rows, cols), 1)
    return jnp.where(pick(r, c), 1.0, 0.0).astype(BF)


def kernel(
    len_ref, q_ref, k_ref, v_ref, cap_ref, img_ref, w_ref,
    gq_ref, gk_ref, gv_ref, gp_ref,
    kvb, qb, dbuf, cbuf, wsend, wz, wbuf,
    bias, pbuf, lowbuf, dsbuf, p2buf, low2buf, ds2buf, atbuf, dob, lse, delta,
    esend, erecv, gacc, dsend, drecv, csend, crecv, asend, gslot, pick,
    dkown, dvown, dqb, dkb, dvb,
    ssem, rsem, lsem,
):
    dp, seq = lax.axis_index("dp"), lax.axis_index("seq")
    c, x = dp % 2, dp // 8
    y, zl = seq % 4, seq // 4
    z = ((dp // 2) % 4) * 2 + zl
    length = len_ref[0]
    mate_z = device(x, y, z + 1 - 2 * zl, c)
    mate_c = device(x, y, z, 1 - c)
    zh = z // 2
    mirror = device(y, x, z, c)
    on_diagonal = x == y
    off_diagonal = x != y
    count = [0]
    groups = []

    class Group:
        def __init__(self, bulk):
            self.slot, self.bulk = count[0], bulk
            count[0] += 1
            groups.append(self)

        def send(self, src, dst, to):
            pltpu.make_async_remote_copy(
                src_ref=src, dst_ref=dst, send_sem=ssem.at[self.slot], recv_sem=rsem.at[self.slot],
                device_id=to, device_id_type=MESH,
            ).start()
            return self

        def whole(self, bulk):
            return pltpu.make_async_remote_copy(
                src_ref=bulk, dst_ref=bulk, send_sem=ssem.at[self.slot], recv_sem=rsem.at[self.slot],
                device_id=mate_c, device_id_type=MESH,
            )

        def arrive(self):
            self.whole(self.bulk).wait_recv()

        def leave(self):
            self.whole(self.bulk).wait_send()

    def at_x(xx):
        return device(xx % 4, y, z, c)

    def at_y(yy):
        return device(x, yy % 4, z, c)

    def at_z(zz):
        return device(x, y, zz % 8, c)

    def cols(index, width):
        return pl.ds(pl.multiple_of(index * width, 128), width)

    def rows(index, height):
        return pl.ds(pl.multiple_of(index * height, height), height)

    barrier = pltpu.get_barrier_semaphore()

    def greet(to):
        pl.semaphore_signal(barrier, inc=1, device_id=to, device_id_type=MESH)

    for i in range(1, 4):
        greet(at_y(y + i))
        greet(at_x(x + i))
    for i in range(1, 8):
        greet(at_z(z + i))
    greet(mate_c)

    @pl.when(off_diagonal)
    def _():
        greet(mirror)

    for h in range(3):
        lane = cols(y * 3 + h, 128)
        pltpu.make_async_copy(k_ref.at[:, lane], kvb.at[h, 0, y, 0], lsem.at[0]).start()
        pltpu.make_async_copy(v_ref.at[:, lane], kvb.at[h, 0, y, 1], lsem.at[0]).start()
    own_q = pltpu.make_async_copy(q_ref.at[:, cols(y, 384)], qb.at[0, y], lsem.at[1])
    own_d = pltpu.make_async_copy(img_ref, dbuf.at[y, pl.ds(16, 112)], lsem.at[2])
    own_c = pltpu.make_async_copy(cap_ref.at[:, cols(y, 384)], cbuf.at[y], lsem.at[3])
    for cp in (own_q, own_d, own_c):
        cp.start()

    w = jnp.concatenate([w_ref[...].astype(F32), jnp.zeros((2, 1536), F32)], axis=0)
    wsend[...] = jnp.concatenate([w[:, j * 384:(j + 1) * 384] for j in range(4)], axis=0).astype(BF)
    dbuf[:, 0:16, :] = jnp.zeros((4, 16, 1536), BF)

    pl.semaphore_wait(barrier, 14 + off_diagonal.astype(jnp.int32))

    wa = Group(wz.at[0])

    @pl.when(off_diagonal)
    def _():
        wa.send(wsend, wz.at[z], mirror)

    @pl.when(on_diagonal)
    def _():
        wz[z] = wsend[...]

    came = [[] for _ in range(3)]

    def exchange(h):
        for i in (1, 3, 2):
            lane = cols((y + i) % 4 * 3 + h, 128)
            source = (y + 4 - i) % 4
            g = Group(kvb.at[h, 0, source])
            g.send(k_ref.at[:, lane], kvb.at[h, 0, y, 0], at_y(y + i))
            g.send(v_ref.at[:, lane], kvb.at[h, 0, y, 1], at_y(y + i))
            came[h].append((source, g))

    far_kv = [Group(kvb.at[h, 1]) for h in range(3)]
    far_q = [Group(qb.at[1, :, :, pl.ds(h * 128, 128)]) for h in range(3)]

    def pass_kv(h, p):
        far_kv[h].send(kvb.at[h, 0, p], kvb.at[h, 1, p], mate_z)

    def pass_q(h):
        lane = pl.ds(h * 128, 128)
        for i in range(4):
            p = (y + i) % 4
            far_q[h].send(qb.at[0, p, :, lane], qb.at[1, p, :, lane], mate_z)

    near_q = [Group(qb.at[0, pl.ds(0, 3), :, pl.ds(h * 128, 128)]) for h in range(3)]
    mine_d = dbuf.at[y, pl.ds(16, 112)]
    from_low, from_high = Group(mine_d), Group(mine_d)

    def exchange_q(h):
        for i in (1, 3, 2):
            lane = cols((y + i) % 4 * 3 + h, 128)
            near_q[h].send(q_ref.at[:, lane], qb.at[0, y, :, pl.ds(h * 128, 128)], at_y(y + i))

    exchange(0)
    own_kv = kvb.at[pl.ds(0, 3), 0, y]
    pltpu.make_async_copy(own_kv, own_kv, lsem.at[0]).wait()
    for h in range(3):
        pass_kv(h, y)
    exchange(1)
    exchange(2)
    exchange_q(0)
    exchange_q(1)
    own_d.wait()
    from_low.send(mine_d, mine_d, at_y(y + 1))
    from_high.send(mine_d, mine_d, at_y(y + 3))
    exchange_q(2)
    caps = Group(cbuf.at[pl.ds(0, 3)])
    for i in range(1, 4):
        caps.send(cap_ref.at[:, cols((y + i) % 4, 384)], cbuf.at[y], at_y(y + i))

    ki = lax.broadcasted_iota(jnp.int32, (1024, 256), 0)
    blk = jnp.where(ki < 512, zl, 1 - zl) * 4 + (ki // 128) % 4
    off = ki % 128
    bias[...] = jnp.where((off < 16) | (blk * 112 + off - 16 < length), 0.0, NEG)

    for half in range(2):
        pick[half] = select(
            192, 384, lambda r, k: k == r % 48 // 12 * 96 + r % 12 // 6 * 24 + r // 48 * 6 + r % 6 + 48 * half
        )

    @pl.when(off_diagonal)
    def _():
        wa.arrive()

    wc = Group(wz.at[pl.ds(0, 7)])
    for i in (4, 3, 5, 2, 6, 1, 7):
        wc.send(wz.at[z], wz.at[z], at_z(z + i))

    def pass_on(h):
        for p, g in came[h]:
            g.arrive()
            pass_kv(h, p)

    pass_on(0)
    pass_on(1)
    pass_on(2)

    wc.arrive()
    squeeze = select(48, 64, lambda r, k: (k % 8 < 6) & (r == k // 8 * 6 + k % 8))
    for j in range(4):
        padded = jnp.concatenate([wz[i].astype(F32)[j * 8:(j + 1) * 8] for i in range(8)], axis=0).astype(BF)
        wbuf[c, x, j] = dot(squeeze, padded, NN).astype(BF)
    quarter = wbuf.at[c, x]
    wd_low = Group(quarter).send(quarter, quarter, at_x(x + 1))
    wd_high = Group(quarter).send(quarter, quarter, at_x(x + 3))

    def whole(buf, h, which):
        return buf[h, :, :, which].reshape(1024, 128)

    def forward(h):
        lanes = slice(h * 128, (h + 1) * 128)
        far_kv[h].arrive()
        kk, vv = whole(kvb, h, 0), whole(kvb, h, 1)
        for t in range(2):
            part = slice(t * 256, (t + 1) * 256)
            qq = qb[0, 2 * t:2 * t + 2, :, lanes].reshape(256, 128)
            s = dot(kk, qq, NT) + bias[...]
            top = jnp.max(s, axis=0, keepdims=True)
            e = jnp.exp2((s - top) * EXP_SCALE)
            total = jnp.sum(e, axis=0, keepdims=True)
            prob = e * (1.0 / total)
            low = prob.astype(BF)
            pbuf[h, :, part] = prob
            lowbuf[h, :, part] = low
            atbuf[lanes, part] = dot(vv, low, TT).astype(BF)
            lse[0, h:h + 1, part] = top * EXP_SCALE + jnp.log2(total)

    own_q.wait()
    near_q[0].arrive()
    pass_q(0)
    forward(0)
    near_q[1].arrive()
    pass_q(1)
    forward(1)
    from_low.arrive()
    from_both = Group(mine_d)
    piece = dbuf.at[(y + 3) % 4, pl.ds(16, 64)]
    from_both.send(piece, piece, at_y(y + 1))
    from_high.arrive()
    piece = dbuf.at[(y + 1) % 4, pl.ds(80, 48)]
    from_both.send(piece, piece, at_y(y + 3))
    wd_both = Group(quarter)
    wd_low.arrive()
    piece = wbuf.at[c, (x + 3) % 4, pl.ds(0, 2)]
    wd_both.send(piece, piece, at_x(x + 1))
    wd_high.arrive()
    piece = wbuf.at[c, (x + 1) % 4, pl.ds(2, 2)]
    wd_both.send(piece, piece, at_x(x + 3))
    near_q[2].arrive()
    pass_q(2)
    forward(2)
    far_lse = Group(lse.at[1]).send(lse.at[0], lse.at[1], mate_z)
    wd_both.arrive()
    we = Group(wbuf.at[c]).send(wbuf.at[c], wbuf.at[c], mate_c)

    qi = lax.broadcasted_iota(jnp.int32, (384, 512), 1)
    off = qi % 128
    token = (zl * 4 + qi // 128) * 112 + off - 16
    at_image = jnp.where((off >= 16) & (token < length), atbuf[...].astype(F32), 0.0)
    at_image = at_image.astype(BF)

    def features(half):
        return dot(pick[half], at_image, NN).astype(BF)

    own_c.wait()
    caps.arrive()
    from_both.arrive()

    def image_cols(j):
        return dbuf[:, :, j * 384:(j + 1) * 384].reshape(512, 384)

    first = features(1 - c)
    for j in range(4):
        esend[:, :, j * 384:(j + 1) * 384] = dot(first, image_cols(j), NN).astype(BF).reshape(4, 48, 384)
    ge = Group(erecv).send(esend, erecv, mate_c)
    second = features(c)
    for j in range(4):
        gacc[:, :, j * 384:(j + 1) * 384] = dot(second, image_cols(j), NN).reshape(4, 48, 384)

    ge.arrive()
    for j in range(4):
        total = gacc[j] + erecv[j].astype(F32)
        gacc[j] = total
        dsend[j] = total.astype(BF)
    gd = Group(drecv)
    for i in (1, 3, 2):
        gd.send(dsend.at[(x + i) % 4], drecv.at[i - 1], at_x(x + i))

    we.arrive()
    do_all = jnp.zeros((512, 384), F32)
    for j in range(4):
        wj = jnp.concatenate([wbuf[i // 4, i % 4, j] for i in range(8)], axis=0)
        do_all += dot(image_cols(j), wj, NT)
    do_all = dot(do_all.astype(BF), pick[...].reshape(384, 384), NN)
    ri = lax.broadcasted_iota(jnp.int32, (512, 384), 0)
    token = (zl * 4 + ri // 128) * 112 + ri % 128 - 16
    do_all = jnp.where(token < length, do_all, 0.0).astype(BF)
    for h in range(3):
        lanes = slice(h * 128, (h + 1) * 128)
        for p in range(4):
            dob[h, 0, p, 0:16] = cbuf[p, :, lanes]
            dob[h, 0, p, 16:128] = do_all[p * 128 + 16:(p + 1) * 128, lanes]
        for t in range(2):
            part = slice(t * 256, (t + 1) * 256)
            do = dob[h, 0, 2 * t:2 * t + 2].reshape(256, 128)
            delta[0, h:h + 1, part] = jnp.sum(
                do.astype(F32).T * atbuf[lanes, part].astype(F32), axis=0, keepdims=True
            )
    far_delta = Group(delta.at[1]).send(delta.at[0], delta.at[1], mate_z)
    far_do = [Group(dob.at[h, 1]).send(dob.at[h, 0], dob.at[h, 1], mate_z) for h in range(3)]

    outs = [(Group(ref.at[:, pl.ds(0, 1152)]), ref, 4 + i) for i, ref in enumerate((gq_ref, gk_ref, gv_ref))]

    def to_rows(src, which, h):
        group, out, sem = outs[which]
        lane = cols(y * 3 + h, 128)
        for i in (1, 3, 2):
            group.send(src.at[h, rows((y + i) % 4, 128)], out.at[:, lane], at_y(y + i))
        pltpu.make_async_copy(src.at[h, rows(y, 128)], out.at[:, lane], lsem.at[sem]).start()

    def backward(h):
        kk, vv = whole(kvb, h, 0), whole(kvb, h, 1)
        for t in range(2):
            part = slice(t * 256, (t + 1) * 256)
            do = dob[h, 0, 2 * t:2 * t + 2].reshape(256, 128)
            dsbuf[:, part] = (pbuf[h, :, part] * (dot(vv, do, NT) - delta[0, h:h + 1, part])).astype(BF)
        dqb[h] = (dot(kk, dsbuf[...], TT) * SCALE).T.astype(BF)
        to_rows(dqb, 0, h)
        lanes = slice(h * 128, (h + 1) * 128)
        dvown[h] = dot(lowbuf[h, 0:512], dob[h, 0].reshape(512, 128), NN)
        dkown[h] = dot(dsbuf[0:512], qb[0, :, :, lanes].reshape(512, 128), NN)

    def far_probs(h):
        lanes = slice(h * 128, (h + 1) * 128)
        kk = kvb[h, 0, :, 0].reshape(512, 128)
        for t in range(2):
            part = slice(t * 256, (t + 1) * 256)
            s = dot(kk, qb[1, 2 * t:2 * t + 2, :, lanes].reshape(256, 128), NT) + bias[0:512]
            prob = jnp.exp2(s * EXP_SCALE - lse[1, h:h + 1, part])
            p2buf[h, :, part] = prob
            low2buf[h, :, part] = prob.astype(BF)

    def far_backward(h):
        lanes = slice(h * 128, (h + 1) * 128)
        far_do[h].arrive()
        vv = kvb[h, 0, :, 1].reshape(512, 128)
        for t in range(2):
            part = slice(t * 256, (t + 1) * 256)
            do = dob[h, 1, 2 * t:2 * t + 2].reshape(256, 128)
            ds2buf[:, part] = (p2buf[h, :, part] * (dot(vv, do, NT) - delta[1, h:h + 1, part])).astype(BF)
        far_qq = qb[1, :, :, lanes].reshape(512, 128)
        dkb[h] = ((dkown[h] + dot(ds2buf[...], far_qq, NN)) * SCALE).astype(BF)
        to_rows(dkb, 1, h)
        dvb[h] = (dvown[h] + dot(low2buf[h], dob[h, 1].reshape(512, 128), NN)).astype(BF)
        to_rows(dvb, 2, h)

    backward(0)
    backward(1)
    backward(2)
    far_lse.arrive()
    for h in range(3):
        far_q[h].arrive()
        far_probs(h)
    far_delta.arrive()
    far_backward(0)
    far_backward(1)

    gd.arrive()
    total = gacc[x] + drecv[0].astype(F32) + drecv[1].astype(F32) + drecv[2].astype(F32)
    spread = select(64, 48, lambda r, k: (r % 8 < 6) & (k == r // 8 * 6 + r % 8))
    total = dot(spread, total.astype(BF), NN)
    for zz in range(8):
        csend[zz] = jnp.concatenate(
            [total[zz * 8:(zz + 1) * 8, j * 384:(j + 1) * 384] for j in range(4)], axis=0
        ).astype(BF)
    gc = Group(crecv)
    for i in (4, 3, 5, 2, 6, 1, 7):
        gc.send(csend.at[(z + i) % 8], crecv.at[i - 1], at_z(z + i))
    far_backward(2)

    gc.arrive()
    total = csend[z].astype(F32)
    for i in range(7):
        total += crecv[i].astype(F32)
    asend[...] = total
    ga = Group(gslot)

    @pl.when(off_diagonal)
    def _():
        ga.send(asend, gslot, mirror)

    @pl.when(on_diagonal)
    def _():
        gslot[...] = total

    for group, out, sem in outs:
        group.arrive()
        bulk = out.at[:, pl.ds(0, 384)]
        pltpu.make_async_copy(bulk, bulk, lsem.at[sem]).wait()
    for group in groups:
        if group not in (wa, ga):
            group.leave()

    @pl.when(off_diagonal)
    def _():
        wa.leave()
        ga.leave()
        ga.arrive()

    for j in range(4):
        gp_ref[:, j * 384:(j + 1) * 384] = gslot[j * 8:j * 8 + 6]
    assert count[0] == SEMS


def copy_out(a, b, c, d, a_out, b_out, c_out, d_out, a_buf, b_buf, c_buf, d_buf, sem):
    chains = ((a, a_buf, a_out), (b, b_buf, b_out), (c, c_buf, c_out), (d, d_buf, d_out))
    reads = [pltpu.make_async_copy(src, buf, sem.at[i]) for i, (src, buf, _) in enumerate(chains)]
    writes = [pltpu.make_async_copy(buf, dst, sem.at[4 + i]) for i, (_, buf, dst) in enumerate(chains)]
    for cp in reads:
        cp.start()
    for read, write in zip(reads, writes):
        read.wait()
        write.start()
    for cp in writes:
        cp.wait()


def shards(query_rows, key_rows, value_rows, d_caption, d_image, proj_weight, lengths):
    block = jax.ShapeDtypeStruct((128, 1536), BF)
    outs = (block, block, block, jax.ShapeDtypeStruct((6, 1536), F32))
    hbm = pl.BlockSpec(memory_space=pl.ANY)
    vmem = pl.BlockSpec(memory_space=pltpu.VMEM)
    scratch = [
        pltpu.VMEM(shape, dtype)
        for shape, dtype in (
            ((3, 2, 4, 2, 128, 128), BF), ((2, 4, 128, 384), BF), ((4, 128, 1536), BF), ((4, 16, 384), BF),
            ((32, 384), BF), ((8, 32, 384), BF), ((2, 4, 4, 48, 384), BF),
            ((1024, 256), F32), ((3, 1024, 512), F32), ((3, 1024, 512), BF), ((1024, 512), BF),
            ((3, 512, 512), F32), ((3, 512, 512), BF), ((512, 512), BF),
            ((384, 512), BF), ((3, 2, 4, 128, 128), BF), ((2, 8, 512), F32), ((2, 8, 512), F32),
            ((4, 48, 1536), BF), ((4, 48, 1536), BF), ((4, 48, 1536), F32), ((4, 48, 1536), BF),
            ((3, 48, 1536), BF), ((8, 32, 384), BF), ((7, 32, 384), BF), ((32, 384), F32), ((32, 384), F32), ((2, 192, 384), BF),
            ((3, 512, 128), F32), ((3, 512, 128), F32),
            ((3, 512, 128), BF), ((3, 512, 128), BF), ((3, 512, 128), BF),
        )
    ]
    results = pl.pallas_call(
        kernel,
        out_shape=outs,
        in_specs=[pl.BlockSpec(memory_space=pltpu.SMEM), hbm, hbm, hbm, hbm, hbm, vmem],
        out_specs=(hbm, hbm, hbm, vmem),
        scratch_shapes=scratch + [
            pltpu.SemaphoreType.DMA((SEMS,)), pltpu.SemaphoreType.DMA((SEMS,)), pltpu.SemaphoreType.DMA((LOCALS,)),
        ],
        compiler_params=pltpu.CompilerParams(
            collective_id=0, has_side_effects=True, vmem_limit_bytes=56 * 2**20
        ),
        name="joint_attention_backward",
    )(lengths, query_rows, key_rows, value_rows, d_caption, d_image, proj_weight)
    return pl.pallas_call(
        copy_out,
        out_shape=outs,
        in_specs=[hbm] * 4,
        out_specs=(hbm,) * 4,
        scratch_shapes=[pltpu.VMEM(o.shape, o.dtype) for o in outs] + [pltpu.SemaphoreType.DMA((8,))],
        name="copy_out",
    )(*results)


def solution(mesh):
    placed = P(("dp", "seq"), None)
    return jax.shard_map(
        shards,
        mesh=mesh,
        in_specs=(placed,) * 6 + (P("dp"),),
        out_specs=(placed,) * 4,
        check_vma=False,
    )
```

```python
import jax
import jax.numpy as jnp
from jax import lax
from jax.experimental import pallas as pl
from jax.experimental.pallas import tpu as pltpu
from jax.sharding import PartitionSpec as P

MESH = pl.DeviceIdType.MESH
F32, BF = jnp.float32, jnp.bfloat16
SCALE = 128 ** (-0.5)
EXP_SCALE = SCALE * 1.4426950408889634
NEG = -1e30
NT = (((1,), (1,)), ((), ()))
TT = (((0,), (0,)), ((), ()))
NN = (((1,), (0,)), ((), ()))
SEMS, LOCALS = 44, 9


def dot(a, b, dims):
    return lax.dot_general(a, b, dims, preferred_element_type=F32)


def device(x, y, z, c):
    return ((x * 4 + z // 2) * 2 + c, (z % 2) * 4 + y)


def select(rows, cols, pick):
    r = lax.broadcasted_iota(jnp.int32, (rows, cols), 0)
    c = lax.broadcasted_iota(jnp.int32, (rows, cols), 1)
    return jnp.where(pick(r, c), 1.0, 0.0).astype(BF)


def kernel(
    len_ref, q_ref, k_ref, v_ref, cap_ref, img_ref, w_ref,
    gq_ref, gk_ref, gv_ref, gp_ref,
    kvb, qb, dbuf, cbuf, wbuf6, wsend, wz, wbuf,
    bias, pbuf, lowbuf, dsbuf, p2buf, low2buf, ds2buf, atbuf, dob, lse, delta,
    esend, erecv, gacc, dsend, drecv, csend, crecv, asend, pick,
    dkown, dvown, dqb, dkb, dvb,
    ssem, rsem, lsem,
):
    dp, seq = lax.axis_index("dp"), lax.axis_index("seq")
    c, x = dp % 2, dp // 8
    y, zl = seq % 4, seq // 4
    z = ((dp // 2) % 4) * 2 + zl
    length = len_ref[0]
    mate_z = device(x, y, z + 1 - 2 * zl, c)
    mate_c = device(x, y, z, 1 - c)
    zh = z // 2
    outer_z = device(x, y, (z + 7 + 2 * zl) % 8, c)
    mirror = device(y, x, z, c)
    zh = z // 2
    on_diagonal = x == y
    off_diagonal = x != y
    count = [0]
    groups = []

    class Group:
        def __init__(self, bulk):
            self.slot, self.bulk = count[0], bulk
            count[0] += 1
            groups.append(self)

        def send(self, src, dst, to):
            pltpu.make_async_remote_copy(
                src_ref=src, dst_ref=dst, send_sem=ssem.at[self.slot], recv_sem=rsem.at[self.slot],
                device_id=to, device_id_type=MESH,
            ).start()
            return self

        def whole(self, bulk):
            return pltpu.make_async_remote_copy(
                src_ref=bulk, dst_ref=bulk, send_sem=ssem.at[self.slot], recv_sem=rsem.at[self.slot],
                device_id=mate_c, device_id_type=MESH,
            )

        def arrive(self):
            self.whole(self.bulk).wait_recv()

        def leave(self):
            self.whole(self.bulk).wait_send()

    def at_x(xx):
        return device(xx % 4, y, z, c)

    def at_y(yy):
        return device(x, yy % 4, z, c)

    def at_z(zz):
        return device(x, y, zz % 8, c)

    def cols(index, width):
        return pl.ds(pl.multiple_of(index * width, 128), width)

    def rows(index, height):
        return pl.ds(pl.multiple_of(index * height, height), height)

    barrier = pltpu.get_barrier_semaphore()

    def greet(to):
        pl.semaphore_signal(barrier, inc=1, device_id=to, device_id_type=MESH)

    for i in range(1, 4):
        greet(at_y(y + i))
        greet(at_x(x + i))
    for i in range(1, 8):
        greet(at_z(z + i))
    greet(mate_c)

    @pl.when(off_diagonal)
    def _():
        greet(mirror)

    own_w = pltpu.make_async_copy(w_ref, wbuf6, lsem.at[7])
    own_w.start()
    for h in range(3):
        lane = cols(y * 3 + h, 128)
        pltpu.make_async_copy(k_ref.at[:, lane], kvb.at[h, 0, y, 0], lsem.at[0]).start()
        pltpu.make_async_copy(v_ref.at[:, lane], kvb.at[h, 0, y, 1], lsem.at[0]).start()
    own_q = pltpu.make_async_copy(q_ref.at[:, cols(y, 384)], qb.at[0, y], lsem.at[1])
    own_d = pltpu.make_async_copy(img_ref, dbuf.at[y, pl.ds(16, 112)], lsem.at[2])
    own_c = pltpu.make_async_copy(cap_ref.at[:, cols(y, 384)], cbuf.at[y], lsem.at[3])
    for cp in (own_q, own_d, own_c):
        cp.start()

    dbuf[:, 0:16, :] = jnp.zeros((4, 16, 1536), BF)

    pl.semaphore_wait(barrier, 14 + off_diagonal.astype(jnp.int32))

    own_w.wait()
    w = jnp.concatenate([wbuf6[...].astype(F32), jnp.zeros((2, 1536), F32)], axis=0)
    wsend[...] = jnp.concatenate([w[:, j * 384:(j + 1) * 384] for j in range(4)], axis=0).astype(BF)
    wa = Group(wz.at[0, 0])

    @pl.when(off_diagonal)
    def _():
        wa.send(wsend, wz.at[zl, zh], mirror)

    @pl.when(on_diagonal)
    def _():
        wz[zl, zh] = wsend[...]

    came = [[] for _ in range(3)]

    def exchange(h):
        for i in (1, 3, 2):
            lane = cols((y + i) % 4 * 3 + h, 128)
            source = (y + 4 - i) % 4
            g = Group(kvb.at[h, 0, source])
            g.send(k_ref.at[:, lane], kvb.at[h, 0, y, 0], at_y(y + i))
            g.send(v_ref.at[:, lane], kvb.at[h, 0, y, 1], at_y(y + i))
            came[h].append((source, g))

    far_kv = [Group(kvb.at[h, 1]) for h in range(3)]
    far_q = [Group(qb.at[1, :, :, pl.ds(h * 128, 128)]) for h in range(3)]

    def pass_kv(h, p):
        far_kv[h].send(kvb.at[h, 0, p], kvb.at[h, 1, p], mate_z)

    def pass_q(h):
        lane = pl.ds(h * 128, 128)
        for i in range(4):
            p = (y + i) % 4
            far_q[h].send(qb.at[0, p, :, lane], qb.at[1, p, :, lane], mate_z)

    near_q = [Group(qb.at[0, pl.ds(0, 3), :, pl.ds(h * 128, 128)]) for h in range(3)]
    mine_d = dbuf.at[y, pl.ds(16, 112)]
    from_low, from_high = Group(mine_d), Group(mine_d)

    def exchange_q(h):
        for i in (1, 3, 2):
            lane = cols((y + i) % 4 * 3 + h, 128)
            near_q[h].send(q_ref.at[:, lane], qb.at[0, y, :, pl.ds(h * 128, 128)], at_y(y + i))

    exchange(0)
    own_kv = kvb.at[pl.ds(0, 3), 0, y]
    pltpu.make_async_copy(own_kv, own_kv, lsem.at[0]).wait()
    for h in range(3):
        pass_kv(h, y)
    exchange(1)
    exchange(2)
    exchange_q(0)
    exchange_q(1)
    own_d.wait()
    from_low.send(mine_d, mine_d, at_y(y + 1))
    from_high.send(mine_d, mine_d, at_y(y + 3))
    exchange_q(2)
    caps = Group(cbuf.at[pl.ds(0, 3)])
    for i in range(1, 4):
        caps.send(cap_ref.at[:, cols((y + i) % 4, 384)], cbuf.at[y], at_y(y + i))

    ki = lax.broadcasted_iota(jnp.int32, (1024, 256), 0)
    blk = jnp.where(ki < 512, zl, 1 - zl) * 4 + (ki // 128) % 4
    off = ki % 128
    bias[...] = jnp.where((off < 16) | (blk * 112 + off - 16 < length), 0.0, NEG)

    for half in range(2):
        pick[half] = select(
            192, 384, lambda r, k: k == r % 48 // 12 * 96 + r % 12 // 6 * 24 + r // 48 * 6 + r % 6 + 48 * half
        )

    @pl.when(off_diagonal)
    def _():
        wa.arrive()

    wc = Group(wz.at[0, pl.ds(0, 3)])
    for i in (2, 1, 3):
        wc.send(wz.at[zl, zh], wz.at[zl, zh], at_z(z + 2 * i))

    def pass_on(h):
        for p, g in came[h]:
            g.arrive()
            pass_kv(h, p)

    pass_on(0)
    pass_on(1)
    wc.arrive()
    wc_outer = Group(wz.at[0]).send(wz.at[zl], wz.at[zl], outer_z)
    pass_on(2)

    wc_outer.arrive()
    squeeze = select(48, 64, lambda r, k: (k % 8 < 6) & (r == k // 8 * 6 + k % 8))
    for j in range(4):
        padded = jnp.concatenate([wz[i % 2, i // 2].astype(F32)[j * 8:(j + 1) * 8] for i in range(8)], axis=0).astype(BF)
        wbuf[c, x, :, j * 384:(j + 1) * 384] = dot(squeeze, padded, NN).astype(BF)
    quarter = wbuf.at[c, x]
    wd_low = Group(quarter).send(quarter, quarter, at_x(x + 1))
    wd_high = Group(quarter).send(quarter, quarter, at_x(x + 3))

    def whole(buf, h, which):
        return buf[h, :, :, which].reshape(1024, 128)

    def forward(h):
        lanes = slice(h * 128, (h + 1) * 128)
        far_kv[h].arrive()
        kk, vv = whole(kvb, h, 0), whole(kvb, h, 1)
        for t in range(2):
            part = slice(t * 256, (t + 1) * 256)
            qq = qb[0, 2 * t:2 * t + 2, :, lanes].reshape(256, 128)
            s = dot(kk, qq, NT) + bias[...]
            top = jnp.max(s, axis=0, keepdims=True)
            e = jnp.exp2((s - top) * EXP_SCALE)
            total = jnp.sum(e, axis=0, keepdims=True)
            prob = e * (1.0 / total)
            low = prob.astype(BF)
            pbuf[h, :, part] = prob
            lowbuf[h, :, part] = low
            atbuf[lanes, part] = dot(vv, low, TT).astype(BF)
            lse[0, h:h + 1, part] = top * EXP_SCALE + jnp.log2(total)

    own_q.wait()
    near_q[0].arrive()
    pass_q(0)
    forward(0)
    near_q[1].arrive()
    pass_q(1)
    forward(1)
    wd_both = Group(quarter)
    wd_low.arrive()
    piece = wbuf.at[c, (x + 3) % 4, :, pl.ds(0, 768)]
    wd_both.send(piece, piece, at_x(x + 1))
    wd_high.arrive()
    piece = wbuf.at[c, (x + 1) % 4, :, pl.ds(768, 768)]
    wd_both.send(piece, piece, at_x(x + 3))
    from_low.arrive()
    from_both = Group(mine_d)
    piece = dbuf.at[(y + 3) % 4, pl.ds(16, 64)]
    from_both.send(piece, piece, at_y(y + 1))
    from_high.arrive()
    piece = dbuf.at[(y + 1) % 4, pl.ds(80, 48)]
    from_both.send(piece, piece, at_y(y + 3))
    wd_both.arrive()
    we = Group(wbuf.at[c]).send(wbuf.at[c], wbuf.at[c], mate_c)
    near_q[2].arrive()
    pass_q(2)
    forward(2)
    far_lse = Group(lse.at[1]).send(lse.at[0], lse.at[1], mate_z)

    far_do = [Group(dob.at[h, 1]) for h in range(3)]
    caps.arrive()
    own_c.wait()
    we.arrive()

    def cotangents(places):
        image = jnp.concatenate([dbuf[p] for p in places], axis=0)
        total = dot(image, wbuf[...].reshape(384, 1536), NT)
        total = dot(total.astype(BF), pick[...].reshape(384, 384), NN)
        off = lax.broadcasted_iota(jnp.int32, (128, 384), 0)
        for n, p in enumerate(places):
            token = (zl * 4 + p) * 112 + off - 16
            part = jnp.where(token < length, total[n * 128:(n + 1) * 128], 0.0).astype(BF)
            for h in range(3):
                lanes = slice(h * 128, (h + 1) * 128)
                dob[h, 0, p, 0:16] = cbuf[p, :, lanes]
                dob[h, 0, p, 16:128] = part[16:128, lanes]

    def pass_do(h, p):
        far_do[h].send(dob.at[h, 0, p], dob.at[h, 1, p], mate_z)

    cotangents([y, (y + 1) % 4, (y + 3) % 4])
    for h in range(2):
        for i in (0, 1, 3):
            pass_do(h, (y + i) % 4)

    qi = lax.broadcasted_iota(jnp.int32, (384, 512), 1)
    off = qi % 128
    token = (zl * 4 + qi // 128) * 112 + off - 16
    at_image = jnp.where((off >= 16) & (token < length), atbuf[...].astype(F32), 0.0)
    at_image = at_image.astype(BF)

    def features(half):
        return dot(pick[half], at_image, NN).astype(BF)

    halves = (slice(0, 768), slice(768, 1536))

    def project(kept, out, part):
        image = dbuf[:, :, part].reshape(512, 768)
        out[:, :, part] = dot(kept, image, NN).astype(out.dtype).reshape(4, 48, 768)

    kept_far, kept_own = features(1 - c), features(c)
    from_both.arrive()

    ge = []
    for part in halves:
        project(kept_far, esend, part)
        lanes = pl.ds(part.start, 768)
        ge.append(Group(erecv.at[:, :, lanes]).send(esend.at[:, :, lanes], erecv.at[:, :, lanes], mate_c))
    for part in halves:
        project(kept_own, gacc, part)
    gd = []
    for part, half in zip(halves, ge):
        half.arrive()
        total = gacc[:, :, part] + erecv[:, :, part].astype(F32)
        gacc[:, :, part] = total
        dsend[:, :, part] = total.astype(BF)
        lanes = pl.ds(part.start, 768)
        gd.append(Group(drecv.at[:, :, lanes]))
        for i in (1, 3, 2):
            gd[-1].send(dsend.at[(x + i) % 4, :, lanes], drecv.at[i - 1, :, lanes], at_x(x + i))

    cotangents([(y + 2) % 4])

    for h in range(3):
        lanes = slice(h * 128, (h + 1) * 128)
        for t in range(2):
            part = slice(t * 256, (t + 1) * 256)
            do = dob[h, 0, 2 * t:2 * t + 2].reshape(256, 128)
            delta[0, h:h + 1, part] = jnp.sum(
                do.astype(F32).T * atbuf[lanes, part].astype(F32), axis=0, keepdims=True
            )
    far_delta = Group(delta.at[1]).send(delta.at[0], delta.at[1], mate_z)
    for h in range(2):
        pass_do(h, (y + 2) % 4)
    far_do[2].send(dob.at[2, 0], dob.at[2, 1], mate_z)

    outs = [(Group(ref.at[:, pl.ds(0, 1152)]), ref, 4 + i) for i, ref in enumerate((gq_ref, gk_ref, gv_ref))]

    def to_rows(src, which, h):
        group, out, sem = outs[which]
        lane = cols(y * 3 + h, 128)
        for i in (1, 3, 2):
            group.send(src.at[h, rows((y + i) % 4, 128)], out.at[:, lane], at_y(y + i))
        pltpu.make_async_copy(src.at[h, rows(y, 128)], out.at[:, lane], lsem.at[sem]).start()

    def backward(h):
        kk, vv = whole(kvb, h, 0), whole(kvb, h, 1)
        for t in range(2):
            part = slice(t * 256, (t + 1) * 256)
            do = dob[h, 0, 2 * t:2 * t + 2].reshape(256, 128)
            dsbuf[:, part] = (pbuf[h, :, part] * (dot(vv, do, NT) - delta[0, h:h + 1, part])).astype(BF)
        dqb[h] = (dot(kk, dsbuf[...], TT) * SCALE).T.astype(BF)
        to_rows(dqb, 0, h)
        lanes = slice(h * 128, (h + 1) * 128)
        dvown[h] = dot(lowbuf[h, 0:512], dob[h, 0].reshape(512, 128), NN)
        dkown[h] = dot(dsbuf[0:512], qb[0, :, :, lanes].reshape(512, 128), NN)

    def far_probs(h):
        lanes = slice(h * 128, (h + 1) * 128)
        kk = kvb[h, 0, :, 0].reshape(512, 128)
        for t in range(2):
            part = slice(t * 256, (t + 1) * 256)
            s = dot(kk, qb[1, 2 * t:2 * t + 2, :, lanes].reshape(256, 128), NT) + bias[0:512]
            prob = jnp.exp2(s * EXP_SCALE - lse[1, h:h + 1, part])
            p2buf[h, :, part] = prob
            low2buf[h, :, part] = prob.astype(BF)

    def far_backward(h):
        lanes = slice(h * 128, (h + 1) * 128)
        far_do[h].arrive()
        vv = kvb[h, 0, :, 1].reshape(512, 128)
        for t in range(2):
            part = slice(t * 256, (t + 1) * 256)
            do = dob[h, 1, 2 * t:2 * t + 2].reshape(256, 128)
            ds2buf[:, part] = (p2buf[h, :, part] * (dot(vv, do, NT) - delta[1, h:h + 1, part])).astype(BF)
        far_qq = qb[1, :, :, lanes].reshape(512, 128)
        dkb[h] = ((dkown[h] + dot(ds2buf[...], far_qq, NN)) * SCALE).astype(BF)
        to_rows(dkb, 1, h)
        dvb[h] = (dvown[h] + dot(low2buf[h], dob[h, 1].reshape(512, 128), NN)).astype(BF)
        to_rows(dvb, 2, h)

    backward(0)
    backward(1)
    backward(2)
    far_lse.arrive()
    for h in range(3):
        far_q[h].arrive()
        far_probs(h)
    far_delta.arrive()
    far_backward(0)

    spread = select(64, 48, lambda r, k: (r % 8 < 6) & (k == r // 8 * 6 + r % 8))
    gc = []

    def along_z(n):
        gd[n].arrive()
        part = halves[n]
        total = gacc[x, :, part]
        for i in range(3):
            total += drecv[i, :, part].astype(F32)
        total = dot(spread, total.astype(BF), NN)
        for zz in range(8):
            rows_z = total[zz * 8:(zz + 1) * 8]
            csend[zz, n] = jnp.concatenate([rows_z[:, 0:384], rows_z[:, 384:768]], axis=0).astype(BF)
        gc.append(Group(crecv.at[:, n]))
        for i in (4, 3, 5, 2, 6, 1, 7):
            gc[n].send(csend.at[(z + i) % 8, n], crecv.at[i - 1, n], at_z(z + i))

    along_z(0)
    far_backward(1)
    far_backward(2)
    along_z(1)

    for group in gc:
        group.arrive()
    total = csend[z].astype(F32)
    for i in range(7):
        total += crecv[i].astype(F32)
    total = total.reshape(32, 384)
    asend[...] = total.astype(BF)
    ga = Group(gp_ref)

    @pl.when(off_diagonal)
    def _():
        ga.send(asend, gp_ref, mirror)

    @pl.when(on_diagonal)
    def _():
        pltpu.make_async_copy(asend, gp_ref, lsem.at[8]).start()

    for group, out, sem in outs:
        group.arrive()
        bulk = out.at[:, pl.ds(0, 384)]
        pltpu.make_async_copy(bulk, bulk, lsem.at[sem]).wait()
    for group in groups:
        if group not in (wa, ga):
            group.leave()

    @pl.when(off_diagonal)
    def _():
        wa.leave()
        ga.leave()
        ga.arrive()

    @pl.when(on_diagonal)
    def _():
        pltpu.make_async_copy(asend, gp_ref, lsem.at[8]).wait()

    assert count[0] == SEMS


def copy_out(gq, gk, gv, gp, gq_out, gk_out, gv_out, gp_out, buf, gp_in, sem):
    small = pltpu.make_async_copy(gp, gp_in, sem.at[0])
    small.start()
    pieces = [(n, h, src, dst) for h in range(2) for n, (src, dst) in enumerate(((gq, gq_out), (gk, gk_out), (gv, gv_out)))]
    reads, writes = [], []
    for n, h, src, dst in pieces:
        rows, k = pl.ds(h * 64, 64), 1 + 2 * n + h
        reads.append(pltpu.make_async_copy(src.at[rows], buf.at[n, rows], sem.at[k]))
        writes.append(pltpu.make_async_copy(buf.at[n, rows], dst.at[rows], sem.at[6 + k]))
    for cp in reads:
        cp.start()
    small.wait()
    rows = gp_in[...].astype(F32)
    for j in range(4):
        gp_out[:, j * 384:(j + 1) * 384] = rows[j * 8:j * 8 + 6]
    for read, write in zip(reads, writes):
        read.wait()
        write.start()
    for cp in writes:
        cp.wait()


def shards(query_rows, key_rows, value_rows, d_caption, d_image, proj_weight, lengths):
    block = jax.ShapeDtypeStruct((128, 1536), BF)
    outs = (block, block, block, jax.ShapeDtypeStruct((6, 1536), F32))
    hbm = pl.BlockSpec(memory_space=pl.ANY)
    vmem = pl.BlockSpec(memory_space=pltpu.VMEM)
    scratch = [
        pltpu.VMEM(shape, dtype)
        for shape, dtype in (
            ((3, 2, 4, 2, 128, 128), BF), ((2, 4, 128, 384), BF), ((4, 128, 1536), BF), ((4, 16, 384), BF),
            ((6, 1536), BF), ((32, 384), BF), ((2, 4, 32, 384), BF), ((2, 4, 48, 1536), BF),
            ((1024, 256), F32), ((3, 1024, 512), F32), ((3, 1024, 512), BF), ((1024, 512), BF),
            ((3, 512, 512), F32), ((3, 512, 512), BF), ((512, 512), BF),
            ((384, 512), BF), ((3, 2, 4, 128, 128), BF), ((2, 8, 512), F32), ((2, 8, 512), F32),
            ((4, 48, 1536), BF), ((4, 48, 1536), BF), ((4, 48, 1536), F32), ((4, 48, 1536), BF),
            ((3, 48, 1536), BF), ((8, 2, 16, 384), BF), ((7, 2, 16, 384), BF), ((32, 384), BF), ((2, 192, 384), BF),
            ((3, 512, 128), F32), ((3, 512, 128), F32),
            ((3, 512, 128), BF), ((3, 512, 128), BF), ((3, 512, 128), BF),
        )
    ]
    results = pl.pallas_call(
        kernel,
        out_shape=(block, block, block, jax.ShapeDtypeStruct((32, 384), BF)),
        in_specs=[pl.BlockSpec(memory_space=pltpu.SMEM), hbm, hbm, hbm, hbm, hbm, hbm],
        out_specs=(hbm,) * 4,
        scratch_shapes=scratch + [
            pltpu.SemaphoreType.DMA((SEMS,)), pltpu.SemaphoreType.DMA((SEMS,)), pltpu.SemaphoreType.DMA((LOCALS,)),
        ],
        compiler_params=pltpu.CompilerParams(
            collective_id=0, has_side_effects=True, vmem_limit_bytes=56 * 2**20
        ),
        name="joint_attention_backward",
    )(lengths, query_rows, key_rows, value_rows, d_caption, d_image, proj_weight)
    return pl.pallas_call(
        copy_out,
        out_shape=outs,
        in_specs=[hbm] * 4,
        out_specs=(hbm, hbm, hbm, vmem),
        scratch_shapes=[
            pltpu.VMEM((3, 128, 1536), BF), pltpu.VMEM((32, 384), BF), pltpu.SemaphoreType.DMA((13,)),
        ],
        name="copy_out",
    )(*results)


def solution(mesh):
    placed = P(("dp", "seq"), None)
    return jax.shard_map(
        shards,
        mesh=mesh,
        in_specs=(placed,) * 6 + (P("dp"),),
        out_specs=(placed,) * 4,
        check_vma=False,
    )
```

```python
import jax
import jax.numpy as jnp
from jax import lax
from jax.experimental import pallas as pl
from jax.experimental.pallas import tpu as pltpu
from jax.sharding import PartitionSpec as P

MESH = pl.DeviceIdType.MESH
F32, BF = jnp.float32, jnp.bfloat16
SCALE = 128 ** (-0.5)
EXP_SCALE = SCALE * 1.4426950408889634
NEG = -1e30
NT = (((1,), (1,)), ((), ()))
TT = (((0,), (0,)), ((), ()))
NN = (((1,), (0,)), ((), ()))
SEMS, LOCALS = 44, 10


def dot(a, b, dims):
    return lax.dot_general(a, b, dims, preferred_element_type=F32)


def device(x, y, z, c):
    return ((x * 4 + z // 2) * 2 + c, (z % 2) * 4 + y)


def select(rows, cols, pick):
    r = lax.broadcasted_iota(jnp.int32, (rows, cols), 0)
    c = lax.broadcasted_iota(jnp.int32, (rows, cols), 1)
    return jnp.where(pick(r, c), 1.0, 0.0).astype(BF)


def kernel(
    len_ref, q_ref, k_ref, v_ref, cap_ref, img_ref, w_ref,
    gq_ref, gk_ref, gv_ref, gp_ref,
    len_buf, kvb, qb, dbuf, cbuf, wbuf6, wsend, wz, wbuf,
    bias, pbuf, lowbuf, dsbuf, p2buf, low2buf, ds2buf, atbuf, dob, lse, delta,
    esend, erecv, gacc, dsend, drecv, csend, crecv, asend, pick,
    dkown, dvown, dqb, dkb, dvb,
    ssem, rsem, lsem,
):
    dp, seq = lax.axis_index("dp"), lax.axis_index("seq")
    c, x = dp % 2, dp // 8
    y, zl = seq % 4, seq // 4
    z = ((dp // 2) % 4) * 2 + zl
    mate_z = device(x, y, z + 1 - 2 * zl, c)
    mate_c = device(x, y, z, 1 - c)
    zh = z // 2
    outer_z = device(x, y, (z + 7 + 2 * zl) % 8, c)
    mirror = device(y, x, z, c)
    zh = z // 2
    on_diagonal = x == y
    off_diagonal = x != y
    count = [0]
    groups = []

    class Group:
        def __init__(self, bulk):
            self.slot, self.bulk = count[0], bulk
            count[0] += 1
            groups.append(self)

        def send(self, src, dst, to):
            pltpu.make_async_remote_copy(
                src_ref=src, dst_ref=dst, send_sem=ssem.at[self.slot], recv_sem=rsem.at[self.slot],
                device_id=to, device_id_type=MESH,
            ).start()
            return self

        def whole(self, bulk):
            return pltpu.make_async_remote_copy(
                src_ref=bulk, dst_ref=bulk, send_sem=ssem.at[self.slot], recv_sem=rsem.at[self.slot],
                device_id=mate_c, device_id_type=MESH,
            )

        def arrive(self):
            self.whole(self.bulk).wait_recv()

        def leave(self):
            self.whole(self.bulk).wait_send()

    def at_x(xx):
        return device(xx % 4, y, z, c)

    def at_y(yy):
        return device(x, yy % 4, z, c)

    def at_z(zz):
        return device(x, y, zz % 8, c)

    def cols(index, width):
        return pl.ds(pl.multiple_of(index * width, 128), width)

    def rows(index, height):
        return pl.ds(pl.multiple_of(index * height, height), height)

    barrier = pltpu.get_barrier_semaphore()

    def greet(to):
        pl.semaphore_signal(barrier, inc=1, device_id=to, device_id_type=MESH)

    for i in range(1, 4):
        greet(at_y(y + i))
        greet(at_x(x + i))
    for i in range(1, 8):
        greet(at_z(z + i))
    greet(mate_c)

    @pl.when(off_diagonal)
    def _():
        greet(mirror)

    own_len = pltpu.make_async_copy(len_ref, len_buf, lsem.at[9])
    own_len.start()
    own_w = pltpu.make_async_copy(w_ref, wbuf6, lsem.at[7])
    own_w.start()
    for h in range(3):
        lane = cols(y * 3 + h, 128)
        pltpu.make_async_copy(k_ref.at[:, lane], kvb.at[h, 0, y, 0], lsem.at[0]).start()
        pltpu.make_async_copy(v_ref.at[:, lane], kvb.at[h, 0, y, 1], lsem.at[0]).start()
    own_q = pltpu.make_async_copy(q_ref.at[:, cols(y, 384)], qb.at[0, y], lsem.at[1])
    own_d = pltpu.make_async_copy(img_ref, dbuf.at[y, pl.ds(16, 112)], lsem.at[2])
    own_c = pltpu.make_async_copy(cap_ref.at[:, cols(y, 384)], cbuf.at[y], lsem.at[3])
    for cp in (own_q, own_d, own_c):
        cp.start()

    dbuf[:, 0:16, :] = jnp.zeros((4, 16, 1536), BF)

    pl.semaphore_wait(barrier, 14 + off_diagonal.astype(jnp.int32))

    own_w.wait()
    w = jnp.concatenate([wbuf6[...].astype(F32), jnp.zeros((2, 1536), F32)], axis=0)
    wsend[...] = jnp.concatenate([w[:, j * 384:(j + 1) * 384] for j in range(4)], axis=0).astype(BF)
    wa = Group(wz.at[0, 0])

    @pl.when(off_diagonal)
    def _():
        wa.send(wsend, wz.at[zl, zh], mirror)

    @pl.when(on_diagonal)
    def _():
        wz[zl, zh] = wsend[...]

    came = [[] for _ in range(3)]

    def exchange(h):
        for i in (1, 3, 2):
            lane = cols((y + i) % 4 * 3 + h, 128)
            source = (y + 4 - i) % 4
            g = Group(kvb.at[h, 0, source])
            g.send(k_ref.at[:, lane], kvb.at[h, 0, y, 0], at_y(y + i))
            g.send(v_ref.at[:, lane], kvb.at[h, 0, y, 1], at_y(y + i))
            came[h].append((source, g))

    far_kv = [Group(kvb.at[h, 1]) for h in range(3)]
    far_q = [Group(qb.at[1, :, :, pl.ds(h * 128, 128)]) for h in range(3)]

    def pass_kv(h, p):
        far_kv[h].send(kvb.at[h, 0, p], kvb.at[h, 1, p], mate_z)

    def pass_q(h):
        lane = pl.ds(h * 128, 128)
        for i in range(4):
            p = (y + i) % 4
            far_q[h].send(qb.at[0, p, :, lane], qb.at[1, p, :, lane], mate_z)

    near_q = [Group(qb.at[0, pl.ds(0, 3), :, pl.ds(h * 128, 128)]) for h in range(3)]
    mine_d = dbuf.at[y, pl.ds(16, 112)]
    from_low, from_high = Group(mine_d), Group(mine_d)

    def exchange_q(h):
        for i in (1, 3, 2):
            lane = cols((y + i) % 4 * 3 + h, 128)
            near_q[h].send(q_ref.at[:, lane], qb.at[0, y, :, pl.ds(h * 128, 128)], at_y(y + i))

    exchange(0)
    own_kv = kvb.at[pl.ds(0, 3), 0, y]
    pltpu.make_async_copy(own_kv, own_kv, lsem.at[0]).wait()
    for h in range(3):
        pass_kv(h, y)
    exchange(1)
    exchange(2)
    exchange_q(0)
    exchange_q(1)
    own_d.wait()
    from_low.send(mine_d, mine_d, at_y(y + 1))
    from_high.send(mine_d, mine_d, at_y(y + 3))
    exchange_q(2)
    caps = Group(cbuf.at[pl.ds(0, 3)])
    for i in range(1, 4):
        caps.send(cap_ref.at[:, cols((y + i) % 4, 384)], cbuf.at[y], at_y(y + i))

    own_len.wait()
    length = len_buf[0]
    ki = lax.broadcasted_iota(jnp.int32, (1024, 256), 0)
    blk = jnp.where(ki < 512, zl, 1 - zl) * 4 + (ki // 128) % 4
    off = ki % 128
    bias[...] = jnp.where((off < 16) | (blk * 112 + off - 16 < length), 0.0, NEG)

    for half in range(2):
        pick[half] = select(
            192, 384, lambda r, k: k == r % 48 // 12 * 96 + r % 12 // 6 * 24 + r // 48 * 6 + r % 6 + 48 * half
        )

    @pl.when(off_diagonal)
    def _():
        wa.arrive()

    wc = Group(wz.at[0, pl.ds(0, 3)])
    for i in (2, 1, 3):
        wc.send(wz.at[zl, zh], wz.at[zl, zh], at_z(z + 2 * i))

    def pass_on(h):
        for p, g in came[h]:
            g.arrive()
            pass_kv(h, p)

    pass_on(0)
    pass_on(1)
    wc.arrive()
    wc_outer = Group(wz.at[0]).send(wz.at[zl], wz.at[zl], outer_z)
    pass_on(2)

    wc_outer.arrive()
    squeeze = select(48, 64, lambda r, k: (k % 8 < 6) & (r == k // 8 * 6 + k % 8))
    for j in range(4):
        padded = jnp.concatenate([wz[i % 2, i // 2].astype(F32)[j * 8:(j + 1) * 8] for i in range(8)], axis=0).astype(BF)
        wbuf[c, x, :, j * 384:(j + 1) * 384] = dot(squeeze, padded, NN).astype(BF)
    quarter = wbuf.at[c, x]
    wd_low = Group(quarter).send(quarter, quarter, at_x(x + 1))
    wd_high = Group(quarter).send(quarter, quarter, at_x(x + 3))

    def whole(buf, h, which):
        return buf[h, :, :, which].reshape(1024, 128)

    def forward(h):
        lanes = slice(h * 128, (h + 1) * 128)
        far_kv[h].arrive()
        kk, vv = whole(kvb, h, 0), whole(kvb, h, 1)
        for t in range(2):
            part = slice(t * 256, (t + 1) * 256)
            qq = qb[0, 2 * t:2 * t + 2, :, lanes].reshape(256, 128)
            s = dot(kk, qq, NT) + bias[...]
            top = jnp.max(s, axis=0, keepdims=True)
            e = jnp.exp2((s - top) * EXP_SCALE)
            total = jnp.sum(e, axis=0, keepdims=True)
            prob = e * (1.0 / total)
            low = prob.astype(BF)
            pbuf[h, :, part] = prob
            lowbuf[h, :, part] = low
            atbuf[lanes, part] = dot(vv, low, TT).astype(BF)
            lse[0, h:h + 1, part] = top * EXP_SCALE + jnp.log2(total)

    own_q.wait()
    near_q[0].arrive()
    pass_q(0)
    forward(0)
    near_q[1].arrive()
    pass_q(1)
    forward(1)
    wd_both = Group(quarter)
    wd_low.arrive()
    piece = wbuf.at[c, (x + 3) % 4, :, pl.ds(0, 768)]
    wd_both.send(piece, piece, at_x(x + 1))
    wd_high.arrive()
    piece = wbuf.at[c, (x + 1) % 4, :, pl.ds(768, 768)]
    wd_both.send(piece, piece, at_x(x + 3))
    from_low.arrive()
    from_both = Group(mine_d)
    piece = dbuf.at[(y + 3) % 4, pl.ds(16, 64)]
    from_both.send(piece, piece, at_y(y + 1))
    from_high.arrive()
    piece = dbuf.at[(y + 1) % 4, pl.ds(80, 48)]
    from_both.send(piece, piece, at_y(y + 3))
    wd_both.arrive()
    we = Group(wbuf.at[c]).send(wbuf.at[c], wbuf.at[c], mate_c)
    near_q[2].arrive()
    pass_q(2)
    forward(2)
    far_lse = Group(lse.at[1]).send(lse.at[0], lse.at[1], mate_z)

    far_do = [Group(dob.at[h, 1]) for h in range(3)]
    caps.arrive()
    own_c.wait()
    we.arrive()

    def cotangents(places):
        image = jnp.concatenate([dbuf[p] for p in places], axis=0)
        total = dot(image, wbuf[...].reshape(384, 1536), NT)
        total = dot(total.astype(BF), pick[...].reshape(384, 384), NN)
        off = lax.broadcasted_iota(jnp.int32, (128, 384), 0)
        for n, p in enumerate(places):
            token = (zl * 4 + p) * 112 + off - 16
            part = jnp.where(token < length, total[n * 128:(n + 1) * 128], 0.0).astype(BF)
            for h in range(3):
                lanes = slice(h * 128, (h + 1) * 128)
                dob[h, 0, p, 0:16] = cbuf[p, :, lanes]
                dob[h, 0, p, 16:128] = part[16:128, lanes]

    def pass_do(h, p):
        far_do[h].send(dob.at[h, 0, p], dob.at[h, 1, p], mate_z)

    cotangents([y, (y + 1) % 4, (y + 3) % 4])
    for h in range(2):
        for i in (0, 1, 3):
            pass_do(h, (y + i) % 4)

    qi = lax.broadcasted_iota(jnp.int32, (384, 512), 1)
    off = qi % 128
    token = (zl * 4 + qi // 128) * 112 + off - 16
    at_image = jnp.where((off >= 16) & (token < length), atbuf[...].astype(F32), 0.0)
    at_image = at_image.astype(BF)

    def features(half):
        return dot(pick[half], at_image, NN).astype(BF)

    halves = (slice(0, 768), slice(768, 1536))

    def project(kept, out, part):
        image = dbuf[:, :, part].reshape(512, 768)
        out[:, :, part] = dot(kept, image, NN).astype(out.dtype).reshape(4, 48, 768)

    kept_far, kept_own = features(1 - c), features(c)
    from_both.arrive()

    ge = []
    for part in halves:
        project(kept_far, esend, part)
        lanes = pl.ds(part.start, 768)
        ge.append(Group(erecv.at[:, :, lanes]).send(esend.at[:, :, lanes], erecv.at[:, :, lanes], mate_c))
    for part in halves:
        project(kept_own, gacc, part)
    gd = []
    for part, half in zip(halves, ge):
        half.arrive()
        total = gacc[:, :, part] + erecv[:, :, part].astype(F32)
        gacc[:, :, part] = total
        dsend[:, :, part] = total.astype(BF)
        lanes = pl.ds(part.start, 768)
        gd.append(Group(drecv.at[:, :, lanes]))
        for i in (1, 3, 2):
            gd[-1].send(dsend.at[(x + i) % 4, :, lanes], drecv.at[i - 1, :, lanes], at_x(x + i))

    cotangents([(y + 2) % 4])

    for h in range(3):
        lanes = slice(h * 128, (h + 1) * 128)
        for t in range(2):
            part = slice(t * 256, (t + 1) * 256)
            do = dob[h, 0, 2 * t:2 * t + 2].reshape(256, 128)
            delta[0, h:h + 1, part] = jnp.sum(
                do.astype(F32).T * atbuf[lanes, part].astype(F32), axis=0, keepdims=True
            )
    far_delta = Group(delta.at[1]).send(delta.at[0], delta.at[1], mate_z)
    for h in range(2):
        pass_do(h, (y + 2) % 4)
    far_do[2].send(dob.at[2, 0], dob.at[2, 1], mate_z)

    outs = [(Group(ref.at[:, pl.ds(0, 1152)]), ref, 4 + i) for i, ref in enumerate((gq_ref, gk_ref, gv_ref))]

    def to_rows(src, which, h):
        group, out, sem = outs[which]
        lane = cols(y * 3 + h, 128)
        for i in (1, 3, 2):
            group.send(src.at[h, rows((y + i) % 4, 128)], out.at[:, lane], at_y(y + i))
        pltpu.make_async_copy(src.at[h, rows(y, 128)], out.at[:, lane], lsem.at[sem]).start()

    def backward(h):
        kk, vv = whole(kvb, h, 0), whole(kvb, h, 1)
        for t in range(2):
            part = slice(t * 256, (t + 1) * 256)
            do = dob[h, 0, 2 * t:2 * t + 2].reshape(256, 128)
            dsbuf[:, part] = (pbuf[h, :, part] * (dot(vv, do, NT) - delta[0, h:h + 1, part])).astype(BF)
        dqb[h] = (dot(kk, dsbuf[...], TT) * SCALE).T.astype(BF)
        to_rows(dqb, 0, h)
        lanes = slice(h * 128, (h + 1) * 128)
        dvown[h] = dot(lowbuf[h, 0:512], dob[h, 0].reshape(512, 128), NN)
        dkown[h] = dot(dsbuf[0:512], qb[0, :, :, lanes].reshape(512, 128), NN)

    def far_probs(h):
        lanes = slice(h * 128, (h + 1) * 128)
        kk = kvb[h, 0, :, 0].reshape(512, 128)
        for t in range(2):
            part = slice(t * 256, (t + 1) * 256)
            s = dot(kk, qb[1, 2 * t:2 * t + 2, :, lanes].reshape(256, 128), NT) + bias[0:512]
            prob = jnp.exp2(s * EXP_SCALE - lse[1, h:h + 1, part])
            p2buf[h, :, part] = prob
            low2buf[h, :, part] = prob.astype(BF)

    def far_backward(h):
        lanes = slice(h * 128, (h + 1) * 128)
        far_do[h].arrive()
        vv = kvb[h, 0, :, 1].reshape(512, 128)
        for t in range(2):
            part = slice(t * 256, (t + 1) * 256)
            do = dob[h, 1, 2 * t:2 * t + 2].reshape(256, 128)
            ds2buf[:, part] = (p2buf[h, :, part] * (dot(vv, do, NT) - delta[1, h:h + 1, part])).astype(BF)
        far_qq = qb[1, :, :, lanes].reshape(512, 128)
        dkb[h] = ((dkown[h] + dot(ds2buf[...], far_qq, NN)) * SCALE).astype(BF)
        to_rows(dkb, 1, h)
        dvb[h] = (dvown[h] + dot(low2buf[h], dob[h, 1].reshape(512, 128), NN)).astype(BF)
        to_rows(dvb, 2, h)

    backward(0)
    backward(1)
    backward(2)
    far_lse.arrive()
    for h in range(3):
        far_q[h].arrive()
        far_probs(h)
    far_delta.arrive()
    far_backward(0)

    spread = select(64, 48, lambda r, k: (r % 8 < 6) & (k == r // 8 * 6 + r % 8))
    gc = []

    def along_z(n):
        gd[n].arrive()
        part = halves[n]
        total = gacc[x, :, part]
        for i in range(3):
            total += drecv[i, :, part].astype(F32)
        total = dot(spread, total.astype(BF), NN)
        for zz in range(8):
            rows_z = total[zz * 8:(zz + 1) * 8]
            csend[zz, n] = jnp.concatenate([rows_z[:, 0:384], rows_z[:, 384:768]], axis=0).astype(BF)
        gc.append(Group(crecv.at[:, n]))
        for i in (4, 3, 5, 2, 6, 1, 7):
            gc[n].send(csend.at[(z + i) % 8, n], crecv.at[i - 1, n], at_z(z + i))

    along_z(0)
    far_backward(1)
    far_backward(2)
    along_z(1)

    for group in gc:
        group.arrive()
    total = csend[z].astype(F32)
    for i in range(7):
        total += crecv[i].astype(F32)
    total = total.reshape(32, 384)
    asend[...] = total.astype(BF)
    ga = Group(gp_ref)

    @pl.when(off_diagonal)
    def _():
        ga.send(asend, gp_ref, mirror)

    @pl.when(on_diagonal)
    def _():
        pltpu.make_async_copy(asend, gp_ref, lsem.at[8]).start()

    for group, out, sem in outs:
        group.arrive()
        bulk = out.at[:, pl.ds(0, 384)]
        pltpu.make_async_copy(bulk, bulk, lsem.at[sem]).wait()
    for group in groups:
        if group not in (wa, ga):
            group.leave()

    @pl.when(off_diagonal)
    def _():
        wa.leave()
        ga.leave()
        ga.arrive()

    @pl.when(on_diagonal)
    def _():
        pltpu.make_async_copy(asend, gp_ref, lsem.at[8]).wait()

    assert count[0] == SEMS


def copy_out(gq, gk, gv, gp, gq_out, gk_out, gv_out, gp_out, gp_buf, sem):
    writes = [
        pltpu.make_async_copy(src, dst, sem.at[n])
        for n, (src, dst) in enumerate(((gq, gq_out), (gk, gk_out), (gv, gv_out), (gp_buf, gp_out)))
    ]
    for cp in writes[:3]:
        cp.start()
    rows = gp[...].astype(F32)
    for j in range(4):
        gp_buf[:, j * 384:(j + 1) * 384] = rows[j * 8:j * 8 + 6]
    writes[3].start()
    for cp in writes:
        cp.wait()


def shards(query_rows, key_rows, value_rows, d_caption, d_image, proj_weight, lengths):
    block = jax.ShapeDtypeStruct((128, 1536), BF)
    outs = (block, block, block, jax.ShapeDtypeStruct((6, 1536), F32))
    hbm = pl.BlockSpec(memory_space=pl.ANY)
    vmem = pl.BlockSpec(memory_space=pltpu.VMEM)
    scratch = [
        pltpu.VMEM(shape, dtype)
        for shape, dtype in (
            ((3, 2, 4, 2, 128, 128), BF), ((2, 4, 128, 384), BF), ((4, 128, 1536), BF), ((4, 16, 384), BF),
            ((6, 1536), BF), ((32, 384), BF), ((2, 4, 32, 384), BF), ((2, 4, 48, 1536), BF),
            ((1024, 256), F32), ((3, 1024, 512), F32), ((3, 1024, 512), BF), ((1024, 512), BF),
            ((3, 512, 512), F32), ((3, 512, 512), BF), ((512, 512), BF),
            ((384, 512), BF), ((3, 2, 4, 128, 128), BF), ((2, 8, 512), F32), ((2, 8, 512), F32),
            ((4, 48, 1536), BF), ((4, 48, 1536), BF), ((4, 48, 1536), F32), ((4, 48, 1536), BF),
            ((3, 48, 1536), BF), ((8, 2, 16, 384), BF), ((7, 2, 16, 384), BF), ((32, 384), BF), ((2, 192, 384), BF),
            ((3, 512, 128), F32), ((3, 512, 128), F32),
            ((3, 512, 128), BF), ((3, 512, 128), BF), ((3, 512, 128), BF),
        )
    ]
    results = pl.pallas_call(
        kernel,
        out_shape=(pltpu.VMEM((128, 1536), BF),) * 3 + (pltpu.VMEM((32, 384), BF),),
        in_specs=[pl.BlockSpec(memory_space=pltpu.MemorySpace.HBM)] + [hbm] * 6,
        out_specs=(vmem,) * 4,
        scratch_shapes=[pltpu.SMEM((1,), jnp.int32)] + scratch + [
            pltpu.SemaphoreType.DMA((SEMS,)), pltpu.SemaphoreType.DMA((SEMS,)), pltpu.SemaphoreType.DMA((LOCALS,)),
        ],
        compiler_params=pltpu.CompilerParams(
            collective_id=0, has_side_effects=True, vmem_limit_bytes=56 * 2**20
        ),
        name="joint_attention_backward",
    )(lengths, query_rows, key_rows, value_rows, d_caption, d_image, proj_weight)
    return pl.pallas_call(
        copy_out,
        out_shape=outs,
        in_specs=[vmem] * 4,
        out_specs=(hbm,) * 4,
        scratch_shapes=[pltpu.VMEM((6, 1536), F32), pltpu.SemaphoreType.DMA((4,))],
        name="copy_out",
    )(*(pltpu.with_memory_space_constraint(r, pltpu.VMEM) for r in results))


def solution(mesh):
    placed = P(("dp", "seq"), None)
    return jax.shard_map(
        shards,
        mesh=mesh,
        in_specs=(placed,) * 6 + (P("dp"),),
        out_specs=(placed,) * 4,
        check_vma=False,
    )
```

```python
import jax
import jax.numpy as jnp
from jax import lax
from jax.experimental import pallas as pl
from jax.experimental.pallas import tpu as pltpu
from jax.sharding import PartitionSpec as P

MESH = pl.DeviceIdType.MESH
F32, BF = jnp.float32, jnp.bfloat16
SCALE = 128 ** (-0.5)
EXP_SCALE = SCALE * 1.4426950408889634
NEG = -1e30
NT = (((1,), (1,)), ((), ()))
TT = (((0,), (0,)), ((), ()))
NN = (((1,), (0,)), ((), ()))
SEMS, LOCALS = 42, 10


def dot(a, b, dims):
    return lax.dot_general(a, b, dims, preferred_element_type=F32)


def device(x, y, z, c):
    return ((x * 4 + z // 2) * 2 + c, (z % 2) * 4 + y)


def select(rows, cols, pick):
    r = lax.broadcasted_iota(jnp.int32, (rows, cols), 0)
    c = lax.broadcasted_iota(jnp.int32, (rows, cols), 1)
    return jnp.where(pick(r, c), 1.0, 0.0).astype(BF)


def kernel(
    len_ref, q_ref, k_ref, v_ref, cap_ref, img_ref, w_ref,
    gq_ref, gk_ref, gv_ref, gp_ref,
    len_buf, kvb, qb, dbuf, cbuf, wbuf6, wsend, wz, wbuf,
    bias, pbuf, lowbuf, dsbuf, p2buf, low2buf, ds2buf, atbuf, dob, lse, delta,
    esend, erecv, gacc, dsend, drecv, csend, crecv, asend, pick,
    dkown, dvown, dqb, dkb, dvb,
    ssem, rsem, lsem,
):
    dp, seq = lax.axis_index("dp"), lax.axis_index("seq")
    c, x = dp % 2, dp // 8
    y, zl = seq % 4, seq // 4
    z = ((dp // 2) % 4) * 2 + zl
    mate_z = device(x, y, z + 1 - 2 * zl, c)
    mate_c = device(x, y, z, 1 - c)
    zh = z // 2
    outer_z = device(x, y, (z + 7 + 2 * zl) % 8, c)
    mirror = device(y, x, z, c)
    zh = z // 2
    on_diagonal = x == y
    off_diagonal = x != y
    count = [0]
    groups = []

    class Group:
        def __init__(self, bulk):
            self.slot, self.bulk = count[0], bulk
            count[0] += 1
            groups.append(self)

        def send(self, src, dst, to):
            pltpu.make_async_remote_copy(
                src_ref=src, dst_ref=dst, send_sem=ssem.at[self.slot], recv_sem=rsem.at[self.slot],
                device_id=to, device_id_type=MESH,
            ).start()
            return self

        def whole(self, bulk):
            return pltpu.make_async_remote_copy(
                src_ref=bulk, dst_ref=bulk, send_sem=ssem.at[self.slot], recv_sem=rsem.at[self.slot],
                device_id=mate_c, device_id_type=MESH,
            )

        def arrive(self):
            self.whole(self.bulk).wait_recv()

        def leave(self):
            self.whole(self.bulk).wait_send()

    def at_x(xx):
        return device(xx % 4, y, z, c)

    def at_y(yy):
        return device(x, yy % 4, z, c)

    def at_z(zz):
        return device(x, y, zz % 8, c)

    def cols(index, width):
        return pl.ds(pl.multiple_of(index * width, 128), width)

    def rows(index, height):
        return pl.ds(pl.multiple_of(index * height, height), height)

    barrier = pltpu.get_barrier_semaphore()

    def greet(to):
        pl.semaphore_signal(barrier, inc=1, device_id=to, device_id_type=MESH)

    for i in range(1, 4):
        greet(at_y(y + i))
        greet(at_x(x + i))
    for i in range(1, 8):
        greet(at_z(z + i))
    greet(mate_c)

    @pl.when(off_diagonal)
    def _():
        greet(mirror)

    own_len = pltpu.make_async_copy(len_ref, len_buf, lsem.at[9])
    own_len.start()
    own_w = pltpu.make_async_copy(w_ref, wbuf6, lsem.at[7])
    own_w.start()
    for h in range(3):
        lane = cols(y * 3 + h, 128)
        pltpu.make_async_copy(k_ref.at[:, lane], kvb.at[h, 0, y, 0], lsem.at[0]).start()
        pltpu.make_async_copy(v_ref.at[:, lane], kvb.at[h, 0, y, 1], lsem.at[0]).start()
    own_q = pltpu.make_async_copy(q_ref.at[:, cols(y, 384)], qb.at[0, y], lsem.at[1])
    own_d = pltpu.make_async_copy(img_ref, dbuf.at[y, pl.ds(16, 112)], lsem.at[2])
    own_c = pltpu.make_async_copy(cap_ref.at[:, cols(y, 384)], cbuf.at[y], lsem.at[3])
    for cp in (own_q, own_d, own_c):
        cp.start()

    dbuf[:, 0:16, :] = jnp.zeros((4, 16, 1536), BF)

    pl.semaphore_wait(barrier, 14 + off_diagonal.astype(jnp.int32))

    own_w.wait()
    w = jnp.concatenate([wbuf6[...].astype(F32), jnp.zeros((2, 1536), F32)], axis=0)
    wsend[...] = jnp.concatenate([w[:, j * 384:(j + 1) * 384] for j in range(4)], axis=0).astype(BF)
    wa = Group(wz.at[0, 0])

    @pl.when(off_diagonal)
    def _():
        wa.send(wsend, wz.at[zl, zh], mirror)

    @pl.when(on_diagonal)
    def _():
        wz[zl, zh] = wsend[...]

    came = [[] for _ in range(3)]

    def exchange(h):
        for i in (1, 3, 2):
            lane = cols((y + i) % 4 * 3 + h, 128)
            source = (y + 4 - i) % 4
            g = Group(kvb.at[h, 0, source])
            g.send(k_ref.at[:, lane], kvb.at[h, 0, y, 0], at_y(y + i))
            g.send(v_ref.at[:, lane], kvb.at[h, 0, y, 1], at_y(y + i))
            came[h].append((source, g))

    far_kv = [Group(kvb.at[h, 1]) for h in range(3)]
    far_q = [Group(qb.at[1, :, :, pl.ds(h * 128, 128)]) for h in range(3)]

    def pass_kv(h, p):
        far_kv[h].send(kvb.at[h, 0, p], kvb.at[h, 1, p], mate_z)

    def pass_q(h):
        lane = pl.ds(h * 128, 128)
        for i in range(4):
            p = (y + i) % 4
            far_q[h].send(qb.at[0, p, :, lane], qb.at[1, p, :, lane], mate_z)

    near_q = [Group(qb.at[0, pl.ds(0, 3), :, pl.ds(h * 128, 128)]) for h in range(3)]
    mine_d = dbuf.at[y, pl.ds(16, 112)]
    from_low, from_high = Group(mine_d), Group(mine_d)

    def exchange_q(h):
        for i in (1, 3, 2):
            lane = cols((y + i) % 4 * 3 + h, 128)
            near_q[h].send(q_ref.at[:, lane], qb.at[0, y, :, pl.ds(h * 128, 128)], at_y(y + i))

    exchange(0)
    own_kv = kvb.at[pl.ds(0, 3), 0, y]
    pltpu.make_async_copy(own_kv, own_kv, lsem.at[0]).wait()
    for h in range(3):
        pass_kv(h, y)
    exchange(1)
    exchange(2)
    exchange_q(0)
    exchange_q(1)
    own_d.wait()
    from_low.send(mine_d, mine_d, at_y(y + 1))
    from_high.send(mine_d, mine_d, at_y(y + 3))
    exchange_q(2)
    caps = Group(cbuf.at[pl.ds(0, 3)])
    for i in range(1, 4):
        caps.send(cap_ref.at[:, cols((y + i) % 4, 384)], cbuf.at[y], at_y(y + i))

    own_len.wait()
    length = len_buf[0]
    ki = lax.broadcasted_iota(jnp.int32, (1024, 256), 0)
    blk = jnp.where(ki < 512, zl, 1 - zl) * 4 + (ki // 128) % 4
    off = ki % 128
    bias[...] = jnp.where((off < 16) | (blk * 112 + off - 16 < length), 0.0, NEG)

    for half in range(2):
        pick[half] = select(
            192, 384, lambda r, k: k == r % 48 // 12 * 96 + r % 12 // 6 * 24 + r // 48 * 6 + r % 6 + 48 * half
        )

    @pl.when(off_diagonal)
    def _():
        wa.arrive()

    wc = Group(wz.at[0, pl.ds(0, 3)])
    for i in (2, 1, 3):
        wc.send(wz.at[zl, zh], wz.at[zl, zh], at_z(z + 2 * i))

    def pass_on(h):
        for p, g in came[h]:
            g.arrive()
            pass_kv(h, p)

    pass_on(0)
    pass_on(1)
    wc.arrive()
    wc_outer = Group(wz.at[0]).send(wz.at[zl], wz.at[zl], outer_z)
    pass_on(2)

    wc_outer.arrive()
    squeeze = select(48, 64, lambda r, k: (k % 8 < 6) & (r == k // 8 * 6 + k % 8))
    for j in range(4):
        padded = jnp.concatenate([wz[i % 2, i // 2].astype(F32)[j * 8:(j + 1) * 8] for i in range(8)], axis=0).astype(BF)
        wbuf[c, x, :, j * 384:(j + 1) * 384] = dot(squeeze, padded, NN).astype(BF)
    quarter = wbuf.at[c, x]
    wd = Group(wbuf.at[c, pl.ds(0, 3)])
    for i in (2, 1, 3):
        wd.send(quarter, quarter, at_x(x + i))

    def whole(buf, h, which):
        return buf[h, :, :, which].reshape(1024, 128)

    def forward(h):
        lanes = slice(h * 128, (h + 1) * 128)
        far_kv[h].arrive()
        kk, vv = whole(kvb, h, 0), whole(kvb, h, 1)
        for t in range(2):
            part = slice(t * 256, (t + 1) * 256)
            qq = qb[0, 2 * t:2 * t + 2, :, lanes].reshape(256, 128)
            s = dot(kk, qq, NT) + bias[...]
            top = jnp.max(s, axis=0, keepdims=True)
            e = jnp.exp2((s - top) * EXP_SCALE)
            total = jnp.sum(e, axis=0, keepdims=True)
            prob = e * (1.0 / total)
            low = prob.astype(BF)
            pbuf[h, :, part] = prob
            lowbuf[h, :, part] = low
            atbuf[lanes, part] = dot(vv, low, TT).astype(BF)
            lse[0, h:h + 1, part] = top * EXP_SCALE + jnp.log2(total)

    own_q.wait()
    near_q[0].arrive()
    pass_q(0)
    forward(0)
    near_q[1].arrive()
    pass_q(1)
    forward(1)
    from_low.arrive()
    from_both = Group(mine_d)
    piece = dbuf.at[(y + 3) % 4, pl.ds(16, 64)]
    from_both.send(piece, piece, at_y(y + 1))
    from_high.arrive()
    piece = dbuf.at[(y + 1) % 4, pl.ds(80, 48)]
    from_both.send(piece, piece, at_y(y + 3))
    wd.arrive()
    we = Group(wbuf.at[c]).send(wbuf.at[c], wbuf.at[c], mate_c)
    near_q[2].arrive()
    pass_q(2)
    forward(2)
    far_lse = Group(lse.at[1]).send(lse.at[0], lse.at[1], mate_z)

    qi = lax.broadcasted_iota(jnp.int32, (384, 512), 1)
    off = qi % 128
    token = (zl * 4 + qi // 128) * 112 + off - 16
    at_image = jnp.where((off >= 16) & (token < length), atbuf[...].astype(F32), 0.0)
    at_image = at_image.astype(BF)

    def features(half):
        return dot(pick[half], at_image, NN).astype(BF)

    halves = (slice(0, 768), slice(768, 1536))

    def project(kept, out, part):
        image = dbuf[:, :, part].reshape(512, 768)
        out[:, :, part] = dot(kept, image, NN).astype(out.dtype).reshape(4, 48, 768)

    kept_far, kept_own = features(1 - c), features(c)
    far_do = [Group(dob.at[h, 1]) for h in range(3)]
    caps.arrive()
    own_c.wait()
    we.arrive()

    def cotangents(places):
        image = jnp.concatenate([dbuf[p] for p in places], axis=0)
        total = dot(image, wbuf[...].reshape(384, 1536), NT)
        total = dot(total.astype(BF), pick[...].reshape(384, 384), NN)
        off = lax.broadcasted_iota(jnp.int32, (128, 384), 0)
        for n, p in enumerate(places):
            token = (zl * 4 + p) * 112 + off - 16
            part = jnp.where(token < length, total[n * 128:(n + 1) * 128], 0.0).astype(BF)
            for h in range(3):
                lanes = slice(h * 128, (h + 1) * 128)
                dob[h, 0, p, 0:16] = cbuf[p, :, lanes]
                dob[h, 0, p, 16:128] = part[16:128, lanes]

    def pass_do(h, p):
        far_do[h].send(dob.at[h, 0, p], dob.at[h, 1, p], mate_z)

    cotangents([y, (y + 1) % 4, (y + 3) % 4])
    for h in range(2):
        for i in (0, 1, 3):
            pass_do(h, (y + i) % 4)

    from_both.arrive()

    ge = []
    for part in halves:
        project(kept_far, esend, part)
        lanes = pl.ds(part.start, 768)
        ge.append(Group(erecv.at[:, :, lanes]).send(esend.at[:, :, lanes], erecv.at[:, :, lanes], mate_c))
    for part in halves:
        project(kept_own, gacc, part)
    gd = []
    for part, half in zip(halves, ge):
        half.arrive()
        total = gacc[:, :, part] + erecv[:, :, part].astype(F32)
        gacc[:, :, part] = total
        dsend[:, :, part] = total.astype(BF)
        lanes = pl.ds(part.start, 768)
        gd.append(Group(drecv.at[:, :, lanes]))
        for i in (1, 3, 2):
            gd[-1].send(dsend.at[(x + i) % 4, :, lanes], drecv.at[i - 1, :, lanes], at_x(x + i))

    cotangents([(y + 2) % 4])

    for h in range(3):
        lanes = slice(h * 128, (h + 1) * 128)
        for t in range(2):
            part = slice(t * 256, (t + 1) * 256)
            do = dob[h, 0, 2 * t:2 * t + 2].reshape(256, 128)
            delta[0, h:h + 1, part] = jnp.sum(
                do.astype(F32).T * atbuf[lanes, part].astype(F32), axis=0, keepdims=True
            )
    far_delta = Group(delta.at[1]).send(delta.at[0], delta.at[1], mate_z)
    for h in range(2):
        pass_do(h, (y + 2) % 4)
    far_do[2].send(dob.at[2, 0], dob.at[2, 1], mate_z)

    outs = [(Group(ref.at[:, pl.ds(0, 1152)]), ref, 4 + i) for i, ref in enumerate((gq_ref, gk_ref, gv_ref))]

    def to_rows(src, which, h):
        group, out, sem = outs[which]
        lane = cols(y * 3 + h, 128)
        for i in (1, 3, 2):
            group.send(src.at[h, rows((y + i) % 4, 128)], out.at[:, lane], at_y(y + i))
        pltpu.make_async_copy(src.at[h, rows(y, 128)], out.at[:, lane], lsem.at[sem]).start()

    def backward(h):
        kk, vv = whole(kvb, h, 0), whole(kvb, h, 1)
        for t in range(2):
            part = slice(t * 256, (t + 1) * 256)
            do = dob[h, 0, 2 * t:2 * t + 2].reshape(256, 128)
            dsbuf[:, part] = (pbuf[h, :, part] * (dot(vv, do, NT) - delta[0, h:h + 1, part])).astype(BF)
        dqb[h] = (dot(kk, dsbuf[...], TT) * SCALE).T.astype(BF)
        to_rows(dqb, 0, h)
        lanes = slice(h * 128, (h + 1) * 128)
        dvown[h] = dot(lowbuf[h, 0:512], dob[h, 0].reshape(512, 128), NN)
        dkown[h] = dot(dsbuf[0:512], qb[0, :, :, lanes].reshape(512, 128), NN)

    def far_probs(h):
        far_q[h].arrive()
        lanes = slice(h * 128, (h + 1) * 128)
        kk = kvb[h, 0, :, 0].reshape(512, 128)
        for t in range(2):
            part = slice(t * 256, (t + 1) * 256)
            s = dot(kk, qb[1, 2 * t:2 * t + 2, :, lanes].reshape(256, 128), NT) + bias[0:512]
            prob = jnp.exp2(s * EXP_SCALE - lse[1, h:h + 1, part])
            p2buf[h, :, part] = prob
            low2buf[h, :, part] = prob.astype(BF)

    def far_backward(h):
        lanes = slice(h * 128, (h + 1) * 128)
        far_do[h].arrive()
        vv = kvb[h, 0, :, 1].reshape(512, 128)
        for t in range(2):
            part = slice(t * 256, (t + 1) * 256)
            do = dob[h, 1, 2 * t:2 * t + 2].reshape(256, 128)
            ds2buf[:, part] = (p2buf[h, :, part] * (dot(vv, do, NT) - delta[1, h:h + 1, part])).astype(BF)
        far_qq = qb[1, :, :, lanes].reshape(512, 128)
        dkb[h] = ((dkown[h] + dot(ds2buf[...], far_qq, NN)) * SCALE).astype(BF)
        to_rows(dkb, 1, h)
        dvb[h] = (dvown[h] + dot(low2buf[h], dob[h, 1].reshape(512, 128), NN)).astype(BF)
        to_rows(dvb, 2, h)

    backward(0)
    backward(1)
    backward(2)
    far_lse.arrive()
    for h in range(3):
        far_probs(h)
    far_delta.arrive()
    far_backward(0)

    spread = select(64, 48, lambda r, k: (r % 8 < 6) & (k == r // 8 * 6 + r % 8))
    gc = []

    def along_z(n):
        gd[n].arrive()
        part = halves[n]
        total = gacc[x, :, part]
        for i in range(3):
            total += drecv[i, :, part].astype(F32)
        total = dot(spread, total.astype(BF), NN)
        for zz in range(8):
            rows_z = total[zz * 8:(zz + 1) * 8]
            csend[zz, n] = jnp.concatenate([rows_z[:, 0:384], rows_z[:, 384:768]], axis=0).astype(BF)
        gc.append(Group(crecv.at[:, n]))
        for i in (4, 3, 5, 2, 6, 1, 7):
            gc[n].send(csend.at[(z + i) % 8, n], crecv.at[i - 1, n], at_z(z + i))

    along_z(0)
    far_backward(1)
    along_z(1)
    far_backward(2)

    for group in gc:
        group.arrive()
    total = csend[z].astype(F32)
    for i in range(7):
        total += crecv[i].astype(F32)
    total = total.reshape(32, 384)
    asend[...] = total.astype(BF)
    ga = Group(gp_ref)

    @pl.when(off_diagonal)
    def _():
        ga.send(asend, gp_ref, mirror)

    @pl.when(on_diagonal)
    def _():
        pltpu.make_async_copy(asend, gp_ref, lsem.at[8]).start()

    for group, out, sem in outs:
        group.arrive()
        bulk = out.at[:, pl.ds(0, 384)]
        pltpu.make_async_copy(bulk, bulk, lsem.at[sem]).wait()
    for group in groups:
        if group not in (wa, ga):
            group.leave()

    @pl.when(off_diagonal)
    def _():
        wa.leave()
        ga.leave()
        ga.arrive()

    @pl.when(on_diagonal)
    def _():
        pltpu.make_async_copy(asend, gp_ref, lsem.at[8]).wait()

    assert count[0] == SEMS


def copy_out(gq, gk, gv, gp, gq_out, gk_out, gv_out, gp_out, gp_buf, sem):
    writes = [
        pltpu.make_async_copy(src, dst, sem.at[n])
        for n, (src, dst) in enumerate(((gq, gq_out), (gk, gk_out), (gv, gv_out), (gp_buf, gp_out)))
    ]
    for cp in writes[:3]:
        cp.start()
    rows = gp[...].astype(F32)
    for j in range(4):
        gp_buf[:, j * 384:(j + 1) * 384] = rows[j * 8:j * 8 + 6]
    writes[3].start()
    for cp in writes:
        cp.wait()


def shards(query_rows, key_rows, value_rows, d_caption, d_image, proj_weight, lengths):
    block = jax.ShapeDtypeStruct((128, 1536), BF)
    outs = (block, block, block, jax.ShapeDtypeStruct((6, 1536), F32))
    hbm = pl.BlockSpec(memory_space=pl.ANY)
    vmem = pl.BlockSpec(memory_space=pltpu.VMEM)
    scratch = [
        pltpu.VMEM(shape, dtype)
        for shape, dtype in (
            ((3, 2, 4, 2, 128, 128), BF), ((2, 4, 128, 384), BF), ((4, 128, 1536), BF), ((4, 16, 384), BF),
            ((6, 1536), BF), ((32, 384), BF), ((2, 4, 32, 384), BF), ((2, 4, 48, 1536), BF),
            ((1024, 256), F32), ((3, 1024, 512), F32), ((3, 1024, 512), BF), ((1024, 512), BF),
            ((3, 512, 512), F32), ((3, 512, 512), BF), ((512, 512), BF),
            ((384, 512), BF), ((3, 2, 4, 128, 128), BF), ((2, 8, 512), F32), ((2, 8, 512), F32),
            ((4, 48, 1536), BF), ((4, 48, 1536), BF), ((4, 48, 1536), F32), ((4, 48, 1536), BF),
            ((3, 48, 1536), BF), ((8, 2, 16, 384), BF), ((7, 2, 16, 384), BF), ((32, 384), BF), ((2, 192, 384), BF),
            ((3, 512, 128), F32), ((3, 512, 128), F32),
            ((3, 512, 128), BF), ((3, 512, 128), BF), ((3, 512, 128), BF),
        )
    ]
    results = pl.pallas_call(
        kernel,
        out_shape=(pltpu.VMEM((128, 1536), BF),) * 3 + (pltpu.VMEM((32, 384), BF),),
        in_specs=[pl.BlockSpec(memory_space=pltpu.MemorySpace.HBM)] + [hbm] * 6,
        out_specs=(vmem,) * 4,
        scratch_shapes=[pltpu.SMEM((1,), jnp.int32)] + scratch + [
            pltpu.SemaphoreType.DMA((SEMS,)), pltpu.SemaphoreType.DMA((SEMS,)), pltpu.SemaphoreType.DMA((LOCALS,)),
        ],
        compiler_params=pltpu.CompilerParams(
            collective_id=0, has_side_effects=True, vmem_limit_bytes=56 * 2**20
        ),
        name="joint_attention_backward",
    )(lengths, query_rows, key_rows, value_rows, d_caption, d_image, proj_weight)
    return pl.pallas_call(
        copy_out,
        out_shape=outs,
        in_specs=[vmem] * 4,
        out_specs=(hbm,) * 4,
        scratch_shapes=[pltpu.VMEM((6, 1536), F32), pltpu.SemaphoreType.DMA((4,))],
        name="copy_out",
    )(*(pltpu.with_memory_space_constraint(r, pltpu.VMEM) for r in results))


def solution(mesh):
    placed = P(("dp", "seq"), None)
    return jax.shard_map(
        shards,
        mesh=mesh,
        in_specs=(placed,) * 6 + (P("dp"),),
        out_specs=(placed,) * 4,
        check_vma=False,
    )
```

```python
import jax
import jax.numpy as jnp
from jax import lax
from jax.experimental import pallas as pl
from jax.experimental.pallas import tpu as pltpu
from jax.sharding import PartitionSpec as P

MESH = pl.DeviceIdType.MESH
F32, BF = jnp.float32, jnp.bfloat16
SCALE = 128 ** (-0.5)
EXP_SCALE = SCALE * 1.4426950408889634
NEG = -1e30
NT = (((1,), (1,)), ((), ()))
TT = (((0,), (0,)), ((), ()))
NN = (((1,), (0,)), ((), ()))
SEMS, SEND_SEMS, LOCALS = 42, 19, 10


def dot(a, b, dims):
    return lax.dot_general(a, b, dims, preferred_element_type=F32)


def device(x, y, z, c):
    return ((x * 4 + z // 2) * 2 + c, (z % 2) * 4 + y)


def select(rows, cols, pick):
    r = lax.broadcasted_iota(jnp.int32, (rows, cols), 0)
    c = lax.broadcasted_iota(jnp.int32, (rows, cols), 1)
    return jnp.where(pick(r, c), 1.0, 0.0).astype(BF)


def kernel(
    len_ref, q_ref, k_ref, v_ref, cap_ref, img_ref, w_ref,
    gq_ref, gk_ref, gv_ref, gp_ref,
    len_buf, kvb, qb, dbuf, cbuf, wbuf6, wsend, wz, wbuf,
    bias, pbuf, lowbuf, dsbuf, p2buf, low2buf, ds2buf, atbuf, dob, lse, delta,
    esend, erecv, gacc, dsend, drecv, csend, crecv, asend, pick,
    dkown, dvown, dqb, dkb, dvb,
    ssem, rsem, lsem,
):
    dp, seq = lax.axis_index("dp"), lax.axis_index("seq")
    c, x = dp % 2, dp // 8
    y, zl = seq % 4, seq // 4
    z = ((dp // 2) % 4) * 2 + zl
    mate_z = device(x, y, z + 1 - 2 * zl, c)
    mate_c = device(x, y, z, 1 - c)
    zh = z // 2
    outer_z = device(x, y, (z + 7 + 2 * zl) % 8, c)
    mirror = device(y, x, z, c)
    zh = z // 2
    on_diagonal = x == y
    off_diagonal = x != y
    count = [0, 0]
    pools = []

    def whole_copy(bulk, send_slot, recv_slot):
        return pltpu.make_async_remote_copy(
            src_ref=bulk, dst_ref=bulk, send_sem=ssem.at[send_slot], recv_sem=rsem.at[recv_slot],
            device_id=mate_c, device_id_type=MESH,
        )

    class Pool:
        def __init__(self, bulk, kept=True):
            self.slot, self.bulk = count[1], bulk
            count[1] += 1
            if kept:
                pools.append(self)

        def leave(self):
            whole_copy(self.bulk, self.slot, 0).wait_send()

    class Group:
        def __init__(self, bulk, pool=None):
            self.slot, self.bulk = count[0], bulk
            self.pool = pool or Pool(bulk)
            count[0] += 1

        def send(self, src, dst, to):
            pltpu.make_async_remote_copy(
                src_ref=src, dst_ref=dst, send_sem=ssem.at[self.pool.slot], recv_sem=rsem.at[self.slot],
                device_id=to, device_id_type=MESH,
            ).start()
            return self

        def arrive(self):
            whole_copy(self.bulk, self.pool.slot, self.slot).wait_recv()

    def at_x(xx):
        return device(xx % 4, y, z, c)

    def at_y(yy):
        return device(x, yy % 4, z, c)

    def at_z(zz):
        return device(x, y, zz % 8, c)

    def cols(index, width):
        return pl.ds(pl.multiple_of(index * width, 128), width)

    def rows(index, height):
        return pl.ds(pl.multiple_of(index * height, height), height)

    barrier = pltpu.get_barrier_semaphore()

    def greet(to):
        pl.semaphore_signal(barrier, inc=1, device_id=to, device_id_type=MESH)

    for i in range(1, 4):
        greet(at_y(y + i))
        greet(at_x(x + i))
    for i in range(1, 8):
        greet(at_z(z + i))
    greet(mate_c)

    @pl.when(off_diagonal)
    def _():
        greet(mirror)

    own_len = pltpu.make_async_copy(len_ref, len_buf, lsem.at[9])
    own_len.start()
    own_w = pltpu.make_async_copy(w_ref, wbuf6, lsem.at[7])
    own_w.start()
    for h in range(3):
        lane = cols(y * 3 + h, 128)
        pltpu.make_async_copy(k_ref.at[:, lane], kvb.at[h, 0, y, 0], lsem.at[0]).start()
        pltpu.make_async_copy(v_ref.at[:, lane], kvb.at[h, 0, y, 1], lsem.at[0]).start()
    own_q = pltpu.make_async_copy(q_ref.at[:, cols(y, 384)], qb.at[0, y], lsem.at[1])
    own_d = pltpu.make_async_copy(img_ref, dbuf.at[y, pl.ds(16, 112)], lsem.at[2])
    own_c = pltpu.make_async_copy(cap_ref.at[:, cols(y, 384)], cbuf.at[y], lsem.at[3])
    for cp in (own_q, own_d, own_c):
        cp.start()

    dbuf[:, 0:16, :] = jnp.zeros((4, 16, 1536), BF)

    pl.semaphore_wait(barrier, 14 + off_diagonal.astype(jnp.int32))

    own_w.wait()
    w = jnp.concatenate([wbuf6[...].astype(F32), jnp.zeros((2, 1536), F32)], axis=0)
    wsend[...] = jnp.concatenate([w[:, j * 384:(j + 1) * 384] for j in range(4)], axis=0).astype(BF)
    wa = Group(wz.at[0, 0], Pool(wz.at[0, 0], False))

    @pl.when(off_diagonal)
    def _():
        wa.send(wsend, wz.at[zl, zh], mirror)

    @pl.when(on_diagonal)
    def _():
        wz[zl, zh] = wsend[...]

    came = [[] for _ in range(3)]
    kv_out, far_out = Pool(kvb.at[:, 0, pl.ds(0, 3)]), Pool(kvb)
    q_out, image_out = Pool(qb.at[0, pl.ds(0, 3)]), Pool(dbuf.at[pl.ds(0, 3), pl.ds(16, 112)])
    stat_out, grad_out = Pool(lse), Pool(low2buf.at[:, pl.ds(0, 288)])

    def exchange(h):
        for i in (1, 3, 2):
            lane = cols((y + i) % 4 * 3 + h, 128)
            source = (y + 4 - i) % 4
            g = Group(kvb.at[h, 0, source], kv_out)
            g.send(k_ref.at[:, lane], kvb.at[h, 0, y, 0], at_y(y + i))
            g.send(v_ref.at[:, lane], kvb.at[h, 0, y, 1], at_y(y + i))
            came[h].append((source, g))

    far_kv = [Group(kvb.at[h, 1], far_out) for h in range(3)]
    far_q = [Group(qb.at[1, :, :, pl.ds(h * 128, 128)], far_out) for h in range(3)]

    def pass_kv(h, p):
        far_kv[h].send(kvb.at[h, 0, p], kvb.at[h, 1, p], mate_z)

    def pass_q(h):
        lane = pl.ds(h * 128, 128)
        for i in range(4):
            p = (y + i) % 4
            far_q[h].send(qb.at[0, p, :, lane], qb.at[1, p, :, lane], mate_z)

    near_q = [Group(qb.at[0, pl.ds(0, 3), :, pl.ds(h * 128, 128)], q_out) for h in range(3)]
    mine_d = dbuf.at[y, pl.ds(16, 112)]
    from_low, from_high = Group(mine_d, image_out), Group(mine_d, image_out)

    def exchange_q(h):
        for i in (1, 3, 2):
            lane = cols((y + i) % 4 * 3 + h, 128)
            near_q[h].send(q_ref.at[:, lane], qb.at[0, y, :, pl.ds(h * 128, 128)], at_y(y + i))

    exchange(0)
    own_kv = kvb.at[pl.ds(0, 3), 0, y]
    pltpu.make_async_copy(own_kv, own_kv, lsem.at[0]).wait()
    for h in range(3):
        pass_kv(h, y)
    exchange(1)
    exchange(2)
    exchange_q(0)
    exchange_q(1)
    own_d.wait()
    from_low.send(mine_d, mine_d, at_y(y + 1))
    from_high.send(mine_d, mine_d, at_y(y + 3))
    exchange_q(2)
    caps = Group(cbuf.at[pl.ds(0, 3)])
    for i in range(1, 4):
        caps.send(cap_ref.at[:, cols((y + i) % 4, 384)], cbuf.at[y], at_y(y + i))

    own_len.wait()
    length = len_buf[0]
    ki = lax.broadcasted_iota(jnp.int32, (1024, 256), 0)
    blk = jnp.where(ki < 512, zl, 1 - zl) * 4 + (ki // 128) % 4
    off = ki % 128
    bias[...] = jnp.where((off < 16) | (blk * 112 + off - 16 < length), 0.0, NEG)

    for half in range(2):
        pick[half] = select(
            192, 384, lambda r, k: k == r % 48 // 12 * 96 + r % 12 // 6 * 24 + r // 48 * 6 + r % 6 + 48 * half
        )

    @pl.when(off_diagonal)
    def _():
        wa.arrive()

    wc = Group(wz.at[0, pl.ds(0, 3)])
    for i in (2, 1, 3):
        wc.send(wz.at[zl, zh], wz.at[zl, zh], at_z(z + 2 * i))

    def pass_on(h):
        for p, g in came[h]:
            g.arrive()
            pass_kv(h, p)

    pass_on(0)
    pass_on(1)
    wc.arrive()
    wc_outer = Group(wz.at[0]).send(wz.at[zl], wz.at[zl], outer_z)
    pass_on(2)

    wc_outer.arrive()
    squeeze = select(48, 64, lambda r, k: (k % 8 < 6) & (r == k // 8 * 6 + k % 8))
    for j in range(4):
        padded = jnp.concatenate([wz[i % 2, i // 2].astype(F32)[j * 8:(j + 1) * 8] for i in range(8)], axis=0).astype(BF)
        wbuf[c, x, :, j * 384:(j + 1) * 384] = dot(squeeze, padded, NN).astype(BF)
    quarter = wbuf.at[c, x]
    wd = Group(wbuf.at[c, pl.ds(0, 3)])
    for i in (2, 1, 3):
        wd.send(quarter, quarter, at_x(x + i))

    def whole(buf, h, which):
        return buf[h, :, :, which].reshape(1024, 128)

    def forward(h):
        lanes = slice(h * 128, (h + 1) * 128)
        far_kv[h].arrive()
        kk, vv = whole(kvb, h, 0), whole(kvb, h, 1)
        for t in range(2):
            part = slice(t * 256, (t + 1) * 256)
            qq = qb[0, 2 * t:2 * t + 2, :, lanes].reshape(256, 128)
            s = dot(kk, qq, NT) + bias[...]
            top = jnp.max(s, axis=0, keepdims=True)
            e = jnp.exp2((s - top) * EXP_SCALE)
            total = jnp.sum(e, axis=0, keepdims=True)
            prob = e * (1.0 / total)
            low = prob.astype(BF)
            pbuf[h, :, part] = prob
            lowbuf[h, :, part] = low
            atbuf[lanes, part] = dot(vv, low, TT).astype(BF)
            lse[0, h:h + 1, part] = top * EXP_SCALE + jnp.log2(total)

    own_q.wait()
    near_q[0].arrive()
    pass_q(0)
    forward(0)
    near_q[1].arrive()
    pass_q(1)
    forward(1)
    from_low.arrive()
    from_both = Group(mine_d, image_out)
    piece = dbuf.at[(y + 3) % 4, pl.ds(16, 64)]
    from_both.send(piece, piece, at_y(y + 1))
    from_high.arrive()
    piece = dbuf.at[(y + 1) % 4, pl.ds(80, 48)]
    from_both.send(piece, piece, at_y(y + 3))
    wd.arrive()
    we = Group(wbuf.at[c]).send(wbuf.at[c], wbuf.at[c], mate_c)
    near_q[2].arrive()
    pass_q(2)
    forward(2)
    far_lse = Group(lse.at[1], stat_out).send(lse.at[0], lse.at[1], mate_z)

    qi = lax.broadcasted_iota(jnp.int32, (384, 512), 1)
    off = qi % 128
    token = (zl * 4 + qi // 128) * 112 + off - 16
    at_image = jnp.where((off >= 16) & (token < length), atbuf[...].astype(F32), 0.0)
    at_image = at_image.astype(BF)

    def features(half):
        return dot(pick[half], at_image, NN).astype(BF)

    halves = (slice(0, 768), slice(768, 1536))

    def project(kept, out, part):
        image = dbuf[:, :, part].reshape(512, 768)
        out[:, :, part] = dot(kept, image, NN).astype(out.dtype).reshape(4, 48, 768)

    kept_far, kept_own = features(1 - c), features(c)
    far_do = [Group(dob.at[h, 1], far_out) for h in range(3)]
    caps.arrive()
    own_c.wait()
    we.arrive()

    def cotangents(places):
        image = jnp.concatenate([dbuf[p] for p in places], axis=0)
        total = dot(image, wbuf[...].reshape(384, 1536), NT)
        total = dot(total.astype(BF), pick[...].reshape(384, 384), NN)
        off = lax.broadcasted_iota(jnp.int32, (128, 384), 0)
        for n, p in enumerate(places):
            token = (zl * 4 + p) * 112 + off - 16
            part = jnp.where(token < length, total[n * 128:(n + 1) * 128], 0.0).astype(BF)
            for h in range(3):
                lanes = slice(h * 128, (h + 1) * 128)
                dob[h, 0, p, 0:16] = cbuf[p, :, lanes]
                dob[h, 0, p, 16:128] = part[16:128, lanes]

    def pass_do(h, p):
        far_do[h].send(dob.at[h, 0, p], dob.at[h, 1, p], mate_z)

    cotangents([y, (y + 1) % 4, (y + 3) % 4])
    for h in range(2):
        for i in (0, 1, 3):
            pass_do(h, (y + i) % 4)

    from_both.arrive()

    ge = []
    for part in halves:
        project(kept_far, esend, part)
        lanes = pl.ds(part.start, 768)
        ge.append(Group(erecv.at[:, :, lanes]).send(esend.at[:, :, lanes], erecv.at[:, :, lanes], mate_c))
    for part in halves:
        project(kept_own, gacc, part)
    gd = []
    for part, half in zip(halves, ge):
        half.arrive()
        total = gacc[:, :, part] + erecv[:, :, part].astype(F32)
        gacc[:, :, part] = total
        dsend[:, :, part] = total.astype(BF)
        lanes = pl.ds(part.start, 768)
        gd.append(Group(drecv.at[:, :, lanes]))
        for i in (1, 3, 2):
            gd[-1].send(dsend.at[(x + i) % 4, :, lanes], drecv.at[i - 1, :, lanes], at_x(x + i))

    cotangents([(y + 2) % 4])

    for h in range(3):
        lanes = slice(h * 128, (h + 1) * 128)
        for t in range(2):
            part = slice(t * 256, (t + 1) * 256)
            do = dob[h, 0, 2 * t:2 * t + 2].reshape(256, 128)
            delta[0, h:h + 1, part] = jnp.sum(
                do.astype(F32).T * atbuf[lanes, part].astype(F32), axis=0, keepdims=True
            )
    far_delta = Group(delta.at[1], stat_out).send(delta.at[0], delta.at[1], mate_z)
    for h in range(2):
        pass_do(h, (y + 2) % 4)
    far_do[2].send(dob.at[2, 0], dob.at[2, 1], mate_z)

    outs = [(Group(ref.at[:, pl.ds(0, 1152)], grad_out), ref, 4 + i) for i, ref in enumerate((gq_ref, gk_ref, gv_ref))]

    def to_rows(src, which, h):
        group, out, sem = outs[which]
        lane = cols(y * 3 + h, 128)
        for i in (1, 3, 2):
            group.send(src.at[h, rows((y + i) % 4, 128)], out.at[:, lane], at_y(y + i))
        pltpu.make_async_copy(src.at[h, rows(y, 128)], out.at[:, lane], lsem.at[sem]).start()

    def backward(h):
        kk, vv = whole(kvb, h, 0), whole(kvb, h, 1)
        for t in range(2):
            part = slice(t * 256, (t + 1) * 256)
            do = dob[h, 0, 2 * t:2 * t + 2].reshape(256, 128)
            dsbuf[:, part] = (pbuf[h, :, part] * (dot(vv, do, NT) - delta[0, h:h + 1, part])).astype(BF)
        dqb[h] = (dot(kk, dsbuf[...], TT) * SCALE).T.astype(BF)
        to_rows(dqb, 0, h)
        lanes = slice(h * 128, (h + 1) * 128)
        dvown[h] = dot(lowbuf[h, 0:512], dob[h, 0].reshape(512, 128), NN)
        dkown[h] = dot(dsbuf[0:512], qb[0, :, :, lanes].reshape(512, 128), NN)

    def far_probs(h):
        far_q[h].arrive()
        lanes = slice(h * 128, (h + 1) * 128)
        kk = kvb[h, 0, :, 0].reshape(512, 128)
        for t in range(2):
            part = slice(t * 256, (t + 1) * 256)
            s = dot(kk, qb[1, 2 * t:2 * t + 2, :, lanes].reshape(256, 128), NT) + bias[0:512]
            prob = jnp.exp2(s * EXP_SCALE - lse[1, h:h + 1, part])
            p2buf[h, :, part] = prob
            low2buf[h, :, part] = prob.astype(BF)

    def far_backward(h):
        lanes = slice(h * 128, (h + 1) * 128)
        far_do[h].arrive()
        vv = kvb[h, 0, :, 1].reshape(512, 128)
        for t in range(2):
            part = slice(t * 256, (t + 1) * 256)
            do = dob[h, 1, 2 * t:2 * t + 2].reshape(256, 128)
            ds2buf[:, part] = (p2buf[h, :, part] * (dot(vv, do, NT) - delta[1, h:h + 1, part])).astype(BF)
        far_qq = qb[1, :, :, lanes].reshape(512, 128)
        dkb[h] = ((dkown[h] + dot(ds2buf[...], far_qq, NN)) * SCALE).astype(BF)
        to_rows(dkb, 1, h)
        dvb[h] = (dvown[h] + dot(low2buf[h], dob[h, 1].reshape(512, 128), NN)).astype(BF)
        to_rows(dvb, 2, h)

    backward(0)
    backward(1)
    backward(2)
    far_lse.arrive()
    for h in range(3):
        far_probs(h)
    far_delta.arrive()
    far_backward(0)

    spread = select(64, 48, lambda r, k: (r % 8 < 6) & (k == r // 8 * 6 + r % 8))
    gc = []

    def along_z(n):
        gd[n].arrive()
        part = halves[n]
        total = gacc[x, :, part]
        for i in range(3):
            total += drecv[i, :, part].astype(F32)
        total = dot(spread, total.astype(BF), NN)
        for zz in range(8):
            rows_z = total[zz * 8:(zz + 1) * 8]
            csend[zz, n] = jnp.concatenate([rows_z[:, 0:384], rows_z[:, 384:768]], axis=0).astype(BF)
        gc.append(Group(crecv.at[:, n]))
        for i in (4, 3, 5, 2, 6, 1, 7):
            gc[n].send(csend.at[(z + i) % 8, n], crecv.at[i - 1, n], at_z(z + i))

    along_z(0)
    far_backward(1)
    along_z(1)
    far_backward(2)

    for group in gc:
        group.arrive()
    total = csend[z].astype(F32)
    for i in range(7):
        total += crecv[i].astype(F32)
    total = total.reshape(32, 384)
    asend[...] = total.astype(BF)
    ga = Group(gp_ref, Pool(gp_ref, False))

    @pl.when(off_diagonal)
    def _():
        ga.send(asend, gp_ref, mirror)

    @pl.when(on_diagonal)
    def _():
        pltpu.make_async_copy(asend, gp_ref, lsem.at[8]).start()

    for group, out, sem in outs:
        group.arrive()
        bulk = out.at[:, pl.ds(0, 384)]
        pltpu.make_async_copy(bulk, bulk, lsem.at[sem]).wait()
    for pool in pools:
        pool.leave()

    @pl.when(off_diagonal)
    def _():
        wa.pool.leave()
        ga.pool.leave()
        ga.arrive()

    @pl.when(on_diagonal)
    def _():
        pltpu.make_async_copy(asend, gp_ref, lsem.at[8]).wait()

    assert count == [SEMS, SEND_SEMS]


def copy_out(gq, gk, gv, gp, gq_out, gk_out, gv_out, gp_out, gp_buf, sem):
    writes = [
        pltpu.make_async_copy(src, dst, sem.at[n])
        for n, (src, dst) in enumerate(((gq, gq_out), (gk, gk_out), (gv, gv_out), (gp_buf, gp_out)))
    ]
    for cp in writes[:3]:
        cp.start()
    rows = gp[...].astype(F32)
    for j in range(4):
        gp_buf[:, j * 384:(j + 1) * 384] = rows[j * 8:j * 8 + 6]
    writes[3].start()
    for cp in writes:
        cp.wait()


def shards(query_rows, key_rows, value_rows, d_caption, d_image, proj_weight, lengths):
    block = jax.ShapeDtypeStruct((128, 1536), BF)
    outs = (block, block, block, jax.ShapeDtypeStruct((6, 1536), F32))
    hbm = pl.BlockSpec(memory_space=pl.ANY)
    vmem = pl.BlockSpec(memory_space=pltpu.VMEM)
    scratch = [
        pltpu.VMEM(shape, dtype)
        for shape, dtype in (
            ((3, 2, 4, 2, 128, 128), BF), ((2, 4, 128, 384), BF), ((4, 128, 1536), BF), ((4, 16, 384), BF),
            ((6, 1536), BF), ((32, 384), BF), ((2, 4, 32, 384), BF), ((2, 4, 48, 1536), BF),
            ((1024, 256), F32), ((3, 1024, 512), F32), ((3, 1024, 512), BF), ((1024, 512), BF),
            ((3, 512, 512), F32), ((3, 512, 512), BF), ((512, 512), BF),
            ((384, 512), BF), ((3, 2, 4, 128, 128), BF), ((2, 8, 512), F32), ((2, 8, 512), F32),
            ((4, 48, 1536), BF), ((4, 48, 1536), BF), ((4, 48, 1536), F32), ((4, 48, 1536), BF),
            ((3, 48, 1536), BF), ((8, 2, 16, 384), BF), ((7, 2, 16, 384), BF), ((32, 384), BF), ((2, 192, 384), BF),
            ((3, 512, 128), F32), ((3, 512, 128), F32),
            ((3, 512, 128), BF), ((3, 512, 128), BF), ((3, 512, 128), BF),
        )
    ]
    results = pl.pallas_call(
        kernel,
        out_shape=(pltpu.VMEM((128, 1536), BF),) * 3 + (pltpu.VMEM((32, 384), BF),),
        in_specs=[pl.BlockSpec(memory_space=pltpu.MemorySpace.HBM)] + [hbm] * 6,
        out_specs=(vmem,) * 4,
        scratch_shapes=[pltpu.SMEM((1,), jnp.int32)] + scratch + [
            pltpu.SemaphoreType.DMA((SEND_SEMS,)), pltpu.SemaphoreType.DMA((SEMS,)), pltpu.SemaphoreType.DMA((LOCALS,)),
        ],
        compiler_params=pltpu.CompilerParams(
            collective_id=0, has_side_effects=True, vmem_limit_bytes=56 * 2**20
        ),
        name="joint_attention_backward",
    )(lengths, query_rows, key_rows, value_rows, d_caption, d_image, proj_weight)
    return pl.pallas_call(
        copy_out,
        out_shape=outs,
        in_specs=[vmem] * 4,
        out_specs=(hbm,) * 4,
        scratch_shapes=[pltpu.VMEM((6, 1536), F32), pltpu.SemaphoreType.DMA((4,))],
        name="copy_out",
    )(*(pltpu.with_memory_space_constraint(r, pltpu.VMEM) for r in results))


def solution(mesh):
    placed = P(("dp", "seq"), None)
    return jax.shard_map(
        shards,
        mesh=mesh,
        in_specs=(placed,) * 6 + (P("dp"),),
        out_specs=(placed,) * 4,
        check_vma=False,
    )
```
